128 devices in a mesh: section: 8 (over x, y_lo), tile: 16 (over z, y_hi, core).
Axes of the slice: x: 4, y: 4 (y_hi: 2, y_lo: 2; y = y_hi * 2 + y_lo), z: 4, core: 2. Of those that a mesh axis runs over, the one named last changes fastest.
Arguments:
- latents: bfloat16 [8, 6144, 1536], P('section', 'tile'), may hold values from -6 to 6
- query_key_value_weight: bfloat16 [8, 1536, 4608], P('section'), may hold values from -0.15625 to 0.15625
- output_weight_stack: bfloat16 [8, 1536, 1536], P('section'), may hold values from -0.15625 to 0.15625
- layer_norm_gains: float32 [8, 1536], P('section'), may hold values from 0.5 to 2
- attended_tile_lists: int32 [16, 3], P('tile'), may hold values from 0 to 15, as said below
- neighbour_tile_count: int32 [16], P('tile'), may hold values from 1 to 3
Outputs:
- advanced: bfloat16 [8, 6144, 1536], P('section', 'tile')
The draws below stay inside these ranges and needn't reach their ends.
Inputs may be any that keep to these rules, and one draw needn't show every extreme that they name: `attended_tile_lists`: the tiles listed for tile t lie among the tiles of the index of tile that holds t and of its two neighbours on that axis; the first entry is t itself and the first neighbour_tile_count[t] entries are distinct.
All inputs are finite; a program needn't handle non-finite values.
Results may differ from the reference program's by a relative error of at most 0.02.
Values may be sent and summed in bfloat16 or wider, within the bound.
No kernel may reach another device: no remote copies, remote signals or barrier semaphores. Data moves between devices by JAX's collectives and lax.ppermute only.
A program may use at most 128 MiB of HBM per device.

```python
import math
import jax
import jax.numpy as jnp
from jax import lax

HEADS = 12
HD = 128
D = 1536
TS = 384
TPD = 1
NBR = 3
HOPS = 2
TILES = 16
TOKENS = 6144
N_SECTION = 8
N_TILE = 16


def draw_attended_tile_lists(key, part):
    key = jax.random.fold_in(key, 11)
    owned = jnp.arange(TILES, dtype=jnp.int32)[:, None]
    offset = jnp.arange(3 * TPD, dtype=jnp.int32)[None, :]
    candidate = owned // TPD * TPD - TPD + offset
    inside = (candidate >= 0) & (candidate < TILES)
    random_score = jax.random.randint(key, (TILES, 3 * TPD), 0, 2 ** 16, dtype=jnp.int32)
    ranked = jnp.where(candidate == owned, 2 ** 17, jnp.where(inside, random_score, -1))
    ranked = ranked * 64 + offset
    ignored, picked = lax.top_k(ranked, NBR)
    chosen = jnp.take_along_axis(candidate, picked, axis=1)
    usable = jnp.take_along_axis(inside, picked, axis=1)
    return jnp.where(usable, chosen, owned).astype(jnp.int32)


def draw_neighbour_tile_count(key, part):
    key = jax.random.fold_in(key, 23)
    owner = jnp.arange(TILES, dtype=jnp.int32) // TPD
    border = (owner == 0) | (owner == N_TILE - 1)
    usable = jnp.where(border, 2 * TPD, 3 * TPD)
    counted = jax.random.randint(key, (TILES,), 1, NBR + 1, dtype=jnp.int32)
    counted = jnp.minimum(counted, usable)
    counted = counted.at[TILES // 2].set(NBR)
    counted = counted.at[0].set(1)
    return counted.astype(jnp.int32)


def levels(key, shape, pieces, smallest, top_value):
    factor_of, own = 1.0, jax.random.fold_in(key, 6)
    for dim, shards_of in pieces:
        draws = jnp.exp(jax.random.uniform(jax.random.fold_in(own, dim), (shards_of,), jnp.float32, smallest / len(pieces), top_value / len(pieces)))
        factor_of = factor_of * jnp.repeat(draws, shape[dim] // shards_of).reshape([-1 if axis == dim else 1 for axis in range(len(shape))])
    return factor_of


def gaussian(rng, shape, width, reach, split=(), kind=jnp.bfloat16):
    level = levels(rng, shape, split, -0.22, 0.18) if split else 1.0
    drawn = jax.random.normal(rng, shape, jnp.float32) * width * level
    return jnp.minimum(jnp.maximum(drawn, -reach), reach).astype(kind)


def setup_inputs(seed: int = 0) -> dict:
    keys = jax.random.split(jax.random.key(seed), 7)
    latents = gaussian(keys[0], (N_SECTION, TOKENS, D), 1.0, 6.0, ((0, 8), (1, 16)))
    query_key_value_weight = gaussian(keys[1], (N_SECTION, D, 3 * D), D ** -0.5, 0.15625, ((0, 8),))
    output_weight_stack = gaussian(keys[2], (N_SECTION, D, D), D ** -0.5, 0.15625, ((0, 8),))
    layer_norm_gains = jnp.clip(jnp.exp(math.log(2.0) - 1.3862944 * jax.random.uniform(keys[3], (N_SECTION, D), jnp.float32) ** levels(keys[3], (N_SECTION, D), ((0, 8),), -0.2, 0.2)), 0.5, 2.0)
    attended_tile_lists = draw_attended_tile_lists(jax.random.fold_in(keys[6], 71), 0)
    neighbour_tile_count = draw_neighbour_tile_count(jax.random.fold_in(keys[6], 71), 0)
    return {"latents": latents, "query_key_value_weight": query_key_value_weight, "output_weight_stack": output_weight_stack, "layer_norm_gains": layer_norm_gains, "attended_tile_lists": attended_tile_lists, "neighbour_tile_count": neighbour_tile_count}


def normalize(hidden_activations, norm_gain_vector):
    widened = hidden_activations.astype(jnp.float32)
    square = lax.optimization_barrier(jnp.mean(widened * widened, axis=-1, keepdims=True))
    return (widened * lax.rsqrt(square + 1e-06) * norm_gain_vector).astype(jnp.bfloat16)

def softmax_weights(scores, allowed):
    masked = jnp.where(allowed, scores, -jnp.inf)
    highest = lax.optimization_barrier(jnp.max(masked, axis=-1, keepdims=True))
    raised = jnp.exp(masked - highest)
    return (raised / lax.optimization_barrier(jnp.sum(raised, axis=-1, keepdims=True))).astype(jnp.bfloat16)

def diffusion_layer_step(hidden_activations, norm_gain_vector, query_key_value_layer, output_projection_layer, attended_tile_lists, neighbour_tile_count):
    normed = normalize(hidden_activations, norm_gain_vector)
    projected = jnp.dot(normed, query_key_value_layer, preferred_element_type=jnp.float32).astype(jnp.bfloat16)
    query = projected[:, :D].reshape(TILES, TS, HEADS, HD).astype(jnp.float32)
    key_tiles = projected[:, D:2 * D].reshape(TILES, TS, HEADS, HD)
    value_tiles = projected[:, 2 * D:].reshape(TILES, TS, HEADS, HD)
    key_rows = key_tiles[attended_tile_lists].reshape(TILES, NBR * TS, HEADS, HD).astype(jnp.float32)
    value_rows = value_tiles[attended_tile_lists].reshape(TILES, NBR * TS, HEADS, HD).astype(jnp.float32)
    scores = jnp.einsum('tqhd,tkhd->thqk', query, key_rows) * HD ** (-0.5)
    slot_index = jnp.arange(NBR * TS, dtype=jnp.int32) // TS
    allowed = (slot_index[None, :] < neighbour_tile_count[:, None])[:, None, None, :]
    probs = softmax_weights(scores, allowed)
    mixed = jnp.einsum('thqk,tkhd->tqhd', probs.astype(jnp.float32), value_rows)
    mixed = mixed.astype(jnp.bfloat16).reshape(TILES * TS, D)
    update = jnp.dot(mixed, output_projection_layer, preferred_element_type=jnp.float32)
    return (hidden_activations.astype(jnp.float32) + update).astype(jnp.bfloat16)

def reference(latents, query_key_value_weight, output_weight_stack, layer_norm_gains, attended_tile_lists, neighbour_tile_count):
    results = []
    for holder in range(N_SECTION):
        batch_index = (holder - HOPS) % N_SECTION
        hidden_activations = latents[batch_index]
        for passed in range(HOPS):
            layer_position = (batch_index + passed) % N_SECTION
            hidden_activations = diffusion_layer_step(hidden_activations, layer_norm_gains[layer_position], query_key_value_weight[layer_position], output_weight_stack[layer_position], attended_tile_lists, neighbour_tile_count)
        results.append(hidden_activations)
    return jnp.stack(results, axis=0)
```

```python
import functools
import math

import jax
import jax.numpy as jnp
from jax import lax
from jax.experimental import pallas as pl
from jax.experimental.pallas import tpu as pltpu
from jax.sharding import PartitionSpec as P

HEADS = 12
HD = 128
D = 1536
TS = 384
N_TILE = 16
N_SECTION = 8
PAIR = 2 * HD
PAIRS = HEADS // 2
SCALE = HD ** (-0.5) * math.log2(math.e)
OFF = -1e30
BOTH = ("section", "tile")


def normalize(hidden, gain):
    widened = hidden.astype(jnp.float32)
    square = jnp.mean(widened * widened, axis=-1, keepdims=True)
    return (widened * lax.rsqrt(square + 1e-06) * gain).astype(jnp.bfloat16)


def dot(a, b):
    return jnp.dot(a, b, preferred_element_type=jnp.float32)


def dot_t(a, b):
    return lax.dot_general(a, b, (((1,), (1,)), ((), ())), preferred_element_type=jnp.float32)


def near_kernel(flag_ref, own_ref, near_ref, gain_ref, wq_ref, wk_ref, wv_ref, q_ref, o_ref, lse_ref, normed):
    j = pl.program_id(0)

    @pl.when(j == 0)
    def _():
        normed[:TS, :] = normalize(own_ref[...], gain_ref[...])
        normed[TS:, :] = normalize(near_ref[...], gain_ref[...])
        lse_ref[...] = jnp.zeros_like(lse_ref)

    q = dot(normed[:TS, :], wq_ref[...]).astype(jnp.bfloat16)
    k = dot(normed[...], wk_ref[...]).astype(jnp.bfloat16)
    v = dot(normed[...], wv_ref[...]).astype(jnp.bfloat16)
    q_ref[...] = q
    bias = jnp.where(flag_ref[0] > 0, 0.0, OFF)
    lane = lax.broadcasted_iota(jnp.int32, lse_ref.shape, 1)
    for i in range(2):
        cut = slice(i * HD, (i + 1) * HD)
        s = dot_t(q[:, cut], k[:, cut])
        s0, s1 = s[:, :TS], s[:, TS:] + bias
        m = jnp.maximum(jnp.max(s0, axis=1, keepdims=True), jnp.max(s1, axis=1, keepdims=True)) * SCALE
        p0 = jnp.exp2(s0 * SCALE - m)
        p1 = jnp.exp2(s1 * SCALE - m)
        total = jnp.sum(p0, axis=1, keepdims=True) + jnp.sum(p1, axis=1, keepdims=True)
        o = dot(p0.astype(jnp.bfloat16), v[:TS, cut]) + dot(p1.astype(jnp.bfloat16), v[TS:, cut])
        o_ref[:, cut] = o / total
        lse_ref[...] = jnp.where(lane == 2 * j + i, m + jnp.log2(total), lse_ref[...])


def far_kernel(flag_ref, own_ref, far_ref, gain_ref, q_ref, o_ref, lse_ref, wk_ref, wv_ref, wo_hbm, out_ref, normed, mixed, wo, sem):
    j = pl.program_id(0)
    copy = pltpu.make_async_copy(wo_hbm, wo, sem)

    @pl.when(j == 0)
    def _():
        copy.start()
        normed[...] = normalize(far_ref[...], gain_ref[...])

    k = dot(normed[...], wk_ref[...]).astype(jnp.bfloat16)
    v = dot(normed[...], wv_ref[...]).astype(jnp.bfloat16)
    bias = jnp.where(flag_ref[0] > 0, 0.0, OFF)
    lane = lax.broadcasted_iota(jnp.int32, lse_ref.shape, 1)
    parts = []
    for i in range(2):
        cut = slice(i * HD, (i + 1) * HD)
        s = dot_t(q_ref[:, cut], k[:, cut]) + bias
        m = jnp.max(s, axis=1, keepdims=True) * SCALE
        p = jnp.exp2(s * SCALE - m)
        total = jnp.sum(p, axis=1, keepdims=True)
        o = dot(p.astype(jnp.bfloat16), v[:, cut])
        before = jnp.sum(jnp.where(lane == 2 * j + i, lse_ref[...], 0.0), axis=1, keepdims=True)
        top = jnp.maximum(before, m)
        w0 = jnp.exp2(before - top)
        w1 = jnp.exp2(m - top)
        r = 1.0 / (w0 + w1 * total)
        parts.append((o_ref[:, cut] * (w0 * r) + o * (w1 * r)).astype(jnp.bfloat16))
    mixed[j] = jnp.concatenate(parts, axis=1)

    @pl.when(j == PAIRS - 1)
    def _():
        copy.wait()
        row = jnp.concatenate([mixed[i] for i in range(PAIRS)], axis=1)
        out_ref[...] = (own_ref[...].astype(jnp.float32) + dot(row, wo[...])).astype(jnp.bfloat16)


def smem():
    return pl.BlockSpec(memory_space=pltpu.SMEM)


def whole(shape):
    return pl.BlockSpec(shape, lambda j: (0, 0))


def columns(rows, first):
    return pl.BlockSpec((rows, PAIR), lambda j: (0, first + j))


def near_attention(flag, own, near, gain, wqkv):
    return pl.pallas_call(
        near_kernel,
        grid=(PAIRS,),
        out_shape=(
            jax.ShapeDtypeStruct((TS, D), jnp.bfloat16),
            jax.ShapeDtypeStruct((TS, D), jnp.float32),
            jax.ShapeDtypeStruct((TS, HD), jnp.float32),
        ),
        in_specs=[
            smem(),
            whole((TS, D)),
            whole((TS, D)),
            whole((1, D)),
            columns(D, 0),
            columns(D, PAIRS),
            columns(D, 2 * PAIRS),
        ],
        out_specs=(columns(TS, 0), columns(TS, 0), whole((TS, HD))),
        scratch_shapes=[pltpu.VMEM((2 * TS, D), jnp.bfloat16)],
        compiler_params=pltpu.CompilerParams(vmem_limit_bytes=40 * 2**20),
        cost_estimate=pl.CostEstimate(flops=13 * 10**9, bytes_accessed=20 * 2**20, transcendentals=4 * 10**6),
        name="near_attention",
    )(flag, own, near, gain, wqkv, wqkv, wqkv)


def far_attention(flag, own, far, gain, q, o, lse, wqkv, wo):
    return pl.pallas_call(
        far_kernel,
        grid=(PAIRS,),
        out_shape=jax.ShapeDtypeStruct((TS, D), jnp.bfloat16),
        in_specs=[
            smem(),
            whole((TS, D)),
            whole((TS, D)),
            whole((1, D)),
            columns(TS, 0),
            columns(TS, 0),
            whole((TS, HD)),
            columns(D, PAIRS),
            columns(D, 2 * PAIRS),
            pl.BlockSpec(memory_space=pl.ANY),
        ],
        out_specs=whole((TS, D)),
        scratch_shapes=[
            pltpu.VMEM((TS, D), jnp.bfloat16),
            pltpu.VMEM((PAIRS, TS, PAIR), jnp.bfloat16),
            pltpu.VMEM((D, D), jnp.bfloat16),
            pltpu.SemaphoreType.DMA,
        ],
        compiler_params=pltpu.CompilerParams(vmem_limit_bytes=40 * 2**20),
        cost_estimate=pl.CostEstimate(flops=8 * 10**9, bytes_accessed=20 * 2**20, transcendentals=2 * 10**6),
        name="far_attention",
    )(flag, own, far, gain, q, o, lse, wqkv, wqkv, wo)


def place(t):
    z, r = divmod(t, 4)
    if r == 0:
        return 4 * ((z - 1) % 4) + 1
    if r == 3:
        return 4 * z
    return 4 * z + 1 + r


def other(t):
    return t + 1 if t % 2 else t - 1


def route(moves):
    return [(s * N_TILE + a, (s + step) % N_SECTION * N_TILE + b) for s in range(N_SECTION) for step, a, b in moves]


TILES = range(N_TILE)
CORE_SWAP = route([(0, t, t ^ 1) for t in TILES])
NEXT_CHIP = route([(0, t, other(t)) for t in TILES if 0 <= other(t) < N_TILE])
FORWARD = route([(1, t, place(t)) for t in TILES])
FORWARD_PAIR = route([(1, t, place(t ^ 1)) for t in TILES])
HOME = route([(1, place(t), t) for t in TILES])
SPREAD = [(t, place(t)) for t in TILES]


def on_device(latents, wqkv, wo, gains, lists, counts):
    own = latents[0]
    wqkv, wo = wqkv[0], wo[0]
    send = functools.partial(lax.ppermute, axis_name=BOTH)
    far = send(own, perm=NEXT_CHIP)
    near = send(own, perm=CORE_SWAP)
    tile = lax.axis_index("tile")
    pair = tile ^ 1
    beyond = jnp.where(tile % 2 == 1, tile + 1, tile - 1)
    used = jnp.arange(lists.shape[1]) < counts[0]
    pair_used = jnp.any((lists[0] == pair) & used).astype(jnp.int32)
    beyond_used = jnp.any((lists[0] == beyond) & used).astype(jnp.int32)
    flags = jnp.stack([pair_used, beyond_used])
    flags_next = lax.ppermute(flags, "tile", SPREAD)

    q, o, lse = near_attention(flags[:1], own, near, gains, wqkv)
    own = far_attention(flags[1:], own, far, gains, q, o, lse, wqkv, wo)
    far = send(own, perm=FORWARD_PAIR)
    own = send(own, perm=FORWARD)
    near = send(own, perm=CORE_SWAP)
    q, o, lse = near_attention(flags_next[1:], own, near, gains, wqkv)
    own = far_attention(flags_next[:1], own, far, gains, q, o, lse, wqkv, wo)
    return send(own, perm=HOME)[None]


def solution(mesh):
    return jax.shard_map(
        on_device,
        mesh=mesh,
        in_specs=(
            P("section", "tile", None),
            P("section", None, None),
            P("section", None, None),
            P("section", None),
            P("tile", None),
            P("tile"),
        ),
        out_specs=P("section", "tile", None),
        check_vma=False,
    )
```

```python
import functools
import math

import jax
import jax.numpy as jnp
from jax import lax
from jax.experimental import pallas as pl
from jax.experimental.pallas import tpu as pltpu
from jax.sharding import PartitionSpec as P

HEADS = 12
HD = 128
D = 1536
TS = 384
HALF = TS // 2
THIRD = TS // 3
N_TILE = 16
N_SECTION = 8
PAIR = 2 * HD
PAIRS = HEADS // 2
SCALE = HD ** (-0.5) * math.log2(math.e)
OFF = -1e30
BOTH = ("section", "tile")
UNROLL = True
NEAR_VMEM = 14 * 2**20
FAR_VMEM = 14 * 2**20
NEAR_FLOPS = 0
FAR_FLOPS = 0


def normalize(hidden, gain):
    widened = hidden.astype(jnp.float32)
    square = jnp.mean(widened * widened, axis=-1, keepdims=True)
    return (widened * lax.rsqrt(square + 1e-06) * gain).astype(jnp.bfloat16)


def dot(a, b):
    return jnp.dot(a, b, preferred_element_type=jnp.float32)


def dot_t(a, b):
    return lax.dot_general(a, b, (((1,), (1,)), ((), ())), preferred_element_type=jnp.float32)


def columns(j, first=0):
    return pl.ds(pl.multiple_of(first + j * PAIR, PAIR), PAIR)


def near_kernel(which, count, flag_ref, own_ref, *refs):
    near_refs, (gain_ref, w_ref, _, q_ref, o_ref, lse_ref, normed, kept_k, kept_v) = refs[:count], refs[count:]
    normed[:TS, :] = normalize(own_ref[...], gain_ref[...])
    rows = TS // count
    for i, ref in enumerate(near_refs):
        normed[TS + i * rows : TS + (i + 1) * rows, :] = normalize(ref[...], gain_ref[...])
    bias = jnp.where(flag_ref[which] > 0, 0.0, OFF)
    lane = lax.broadcasted_iota(jnp.int32, lse_ref.shape, 1)
    lse_ref[...] = jnp.zeros_like(lse_ref)
    for head in range(2):
        kept_v[:, :, head * PAIR + HD : (head + 1) * PAIR] = jnp.ones((2, 2 * TS, HD), jnp.bfloat16)

    def project_q(j):
        q_ref[:, columns(j)] = (dot(normed[:TS, :], w_ref[:, columns(j)]) * SCALE).astype(jnp.bfloat16)

    def project_k(j, slot):
        kept_k[slot] = dot(normed[...], w_ref[:, columns(j, D)]).astype(jnp.bfloat16)

    def project_v(j, slot):
        v = dot(normed[...], w_ref[:, columns(j, 2 * D)]).astype(jnp.bfloat16)
        kept_v[slot, :, :HD] = v[:, :HD]
        kept_v[slot, :, PAIR : PAIR + HD] = v[:, HD:]

    def score(q, k, i):
        return dot_t(q[:, i * HD : (i + 1) * HD], k[:, i * HD : (i + 1) * HD])

    def weigh(s):
        s0, s1 = s[:, :TS], s[:, TS:]
        m = jnp.maximum(jnp.max(s0, axis=1, keepdims=True), jnp.max(s1, axis=1, keepdims=True) + bias)
        p0 = jnp.exp2(s0 - m).astype(jnp.bfloat16)
        p1 = jnp.exp2(s1 - (m - bias)).astype(jnp.bfloat16)
        return jnp.concatenate([p0, p1], axis=1), m

    def collect(p, m, v, j, i):
        mixed = dot(p, v[:, i * PAIR : (i + 1) * PAIR])
        total = mixed[:, HD:]
        first = pl.multiple_of(j * PAIR, PAIR) + i * HD
        o_ref[:, pl.ds(first, HD)] = mixed[:, :HD] / total
        lse_ref[...] = jnp.where(lane == 2 * j + i, m + jnp.log2(total), lse_ref[...])

    project_q(0)
    project_k(0, 0)
    project_v(0, 0)

    def step(j, more):
        slot = j % 2
        q, k, v = q_ref[:, columns(j)], kept_k[slot], kept_v[slot]
        s0 = score(q, k, 0)
        if more:
            project_q(j + 1)
        p0, m0 = weigh(s0)
        s1 = score(q, k, 1)
        if more:
            project_k(j + 1, 1 - slot)
        p1, m1 = weigh(s1)
        collect(p0, m0, v, j, 0)
        if more:
            project_v(j + 1, 1 - slot)
        collect(p1, m1, v, j, 1)

    steps(step)


def steps(step):
    if UNROLL:
        for j in range(PAIRS - 1):
            step(j, True)
    else:
        lax.fori_loop(0, PAIRS - 1, lambda j, carry: step(j, True) or carry, 0)
    step(PAIRS - 1, False)


def far_kernel(which, count, flag_ref, own_ref, *refs):
    far_refs, refs = refs[:count], refs[count:]
    gain_ref, q_ref, o_ref, lse_ref, w_ref, wo_ref, out_ref, normed, mixed, kept_k, kept_v = refs
    rows = TS // count
    for i, ref in enumerate(far_refs):
        normed[i * rows : (i + 1) * rows, :] = normalize(ref[...], gain_ref[...])
    bias = jnp.where(flag_ref[which] > 0, 0.0, OFF)
    lane = lax.broadcasted_iota(jnp.int32, lse_ref.shape, 1)
    for head in range(2):
        kept_v[:, :, head * PAIR + HD : (head + 1) * PAIR] = jnp.ones((2, TS, HD), jnp.bfloat16)

    def project_k(j, slot):
        kept_k[slot] = dot(normed[...], w_ref[:, columns(j, D)]).astype(jnp.bfloat16)

    def project_v(j, slot):
        v = dot(normed[...], w_ref[:, columns(j, 2 * D)]).astype(jnp.bfloat16)
        kept_v[slot, :, :HD] = v[:, :HD]
        kept_v[slot, :, PAIR : PAIR + HD] = v[:, HD:]

    def score(q, k, i):
        return dot_t(q[:, i * HD : (i + 1) * HD], k[:, i * HD : (i + 1) * HD])

    def weigh(s):
        m = jnp.max(s, axis=1, keepdims=True)
        return jnp.exp2(s - m).astype(jnp.bfloat16), m + bias

    def collect(p, m, v, j, i):
        both = dot(p, v[:, i * PAIR : (i + 1) * PAIR])
        before = jnp.sum(jnp.where(lane == 2 * j + i, lse_ref[...], 0.0), axis=1, keepdims=True)
        top = jnp.maximum(before, m)
        w0, w1 = jnp.exp2(before - top), jnp.exp2(m - top)
        first = pl.multiple_of(j * PAIR, PAIR) + i * HD
        o = (o_ref[:, pl.ds(first, HD)] * w0 + both[:, :HD] * w1) / (w0 + both[:, HD:] * w1)
        mixed[:, pl.ds(first, HD)] = o.astype(jnp.bfloat16)

    project_k(0, 0)
    project_v(0, 0)

    def step(j, more):
        slot = j % 2
        q, k, v = q_ref[:, columns(j)], kept_k[slot], kept_v[slot]
        s0 = score(q, k, 0)
        s1 = score(q, k, 1)
        p0, m0 = weigh(s0)
        if more:
            project_k(j + 1, 1 - slot)
        p1, m1 = weigh(s1)
        collect(p0, m0, v, j, 0)
        if more:
            project_v(j + 1, 1 - slot)
        collect(p1, m1, v, j, 1)

    steps(step)

    def finish(j, carry):
        update = dot(mixed[...], wo_ref[:, columns(j)])
        out_ref[:, columns(j)] = (own_ref[:, columns(j)].astype(jnp.float32) + update).astype(jnp.bfloat16)
        return carry

    lax.fori_loop(0, PAIRS, finish, 0, unroll=UNROLL)


SMEM = pl.BlockSpec(memory_space=pltpu.SMEM)
VMEM = pl.BlockSpec(memory_space=pltpu.VMEM)


def near_attention(which, flags, own, near, gain, wqkv, wo):
    return pl.pallas_call(
        functools.partial(near_kernel, which, len(near)),
        out_shape=(
            jax.ShapeDtypeStruct((TS, D), jnp.bfloat16),
            jax.ShapeDtypeStruct((TS, D), jnp.float32),
            jax.ShapeDtypeStruct((TS, HD), jnp.float32),
        ),
        in_specs=[SMEM] + [VMEM] * (4 + len(near)),
        out_specs=(VMEM, VMEM, VMEM),
        scratch_shapes=[
            pltpu.VMEM((2 * TS, D), jnp.bfloat16),
            pltpu.VMEM((2, 2 * TS, PAIR), jnp.bfloat16),
            pltpu.VMEM((2, 2 * TS, 2 * PAIR), jnp.bfloat16),
        ],
        compiler_params=pltpu.CompilerParams(vmem_limit_bytes=NEAR_VMEM),
        cost_estimate=pl.CostEstimate(flops=NEAR_FLOPS, bytes_accessed=0, transcendentals=0),
        name="near_attention",
    )(flags, own, *near, gain, wqkv, wo)


def far_attention(which, flags, own, far, gain, q, o, lse, wqkv, wo):
    return pl.pallas_call(
        functools.partial(far_kernel, which, len(far)),
        out_shape=jax.ShapeDtypeStruct((TS, D), jnp.bfloat16),
        in_specs=[SMEM] + [VMEM] * (7 + len(far)),
        out_specs=VMEM,
        scratch_shapes=[
            pltpu.VMEM((TS, D), jnp.bfloat16),
            pltpu.VMEM((TS, D), jnp.bfloat16),
            pltpu.VMEM((2, TS, PAIR), jnp.bfloat16),
            pltpu.VMEM((2, TS, 2 * PAIR), jnp.bfloat16),
        ],
        compiler_params=pltpu.CompilerParams(vmem_limit_bytes=FAR_VMEM),
        cost_estimate=pl.CostEstimate(flops=FAR_FLOPS, bytes_accessed=0, transcendentals=0),
        name="far_attention",
    )(flags, own, *far, gain, q, o, lse, wqkv, wo)


def place(t):
    z, r = divmod(t, 4)
    if r == 0:
        return 4 * ((z - 1) % 4) + 1
    if r == 3:
        return 4 * z
    return 4 * z + 1 + r


def other(t):
    return t + 1 if t % 2 else t - 1


def route(moves):
    return [(s * N_TILE + a, (s + step) % N_SECTION * N_TILE + b) for s in range(N_SECTION) for step, a, b in moves]


def step_out(s):
    return s + 1 if s % 2 == 0 else s - 1


TILES = range(N_TILE)
CORE_SWAP = route([(0, t, t ^ 1) for t in TILES])
NEXT_CHIP = route([(0, t, other(t)) for t in TILES if 0 <= other(t) < N_TILE])
FORWARD = route([(1, t, place(t)) for t in TILES])
PAIR_OUT = [(s * N_TILE + t, step_out(s) * N_TILE + place(t ^ 1)) for s in range(N_SECTION) for t in TILES]
PAIR_IN = [(step_out(s) * N_TILE + u, (s + 1) % N_SECTION * N_TILE + u) for s in range(N_SECTION) for u in TILES]
HOME = route([(1, place(t), t) for t in TILES])
SPREAD = [(t, place(t)) for t in TILES]


def pieces(block, rows):
    return [block[i : i + rows] for i in range(0, TS, rows)]


def on_device(latents, wqkv, wo, gains, lists, counts):
    own = latents[0]
    wqkv, wo = wqkv[0], wo[0]

    def send(perm, blocks):
        return [lax.ppermute(block, BOTH, perm) for block in blocks]

    far = send(NEXT_CHIP, [own])
    near = send(CORE_SWAP, [own])
    tile = lax.axis_index("tile")
    pair = tile ^ 1
    beyond = jnp.where(tile % 2 == 1, tile + 1, tile - 1)
    used = jnp.arange(lists.shape[1]) < counts[0]
    pair_used = jnp.any((lists[0] == pair) & used).astype(jnp.int32)
    beyond_used = jnp.any((lists[0] == beyond) & used).astype(jnp.int32)
    flags = jnp.stack([pair_used, beyond_used])

    q, o, lse = near_attention(0, flags, own, near, gains, wqkv, wo)
    flags, lse = lax.optimization_barrier((flags, lse))
    flags_next = lax.ppermute(flags, "tile", SPREAD)
    flags, flags_next = lax.optimization_barrier((flags, flags_next))
    own = far_attention(1, flags, own, far, gains, q, o, lse, wqkv, wo)
    far = send(PAIR_IN, send(PAIR_OUT, pieces(own, HALF)))
    (own,) = send(FORWARD, [own])
    near = send(CORE_SWAP, pieces(own, THIRD))
    q, o, lse = near_attention(1, flags_next, own, near, gains, wqkv, wo)
    own = far_attention(0, flags_next, own, far, gains, q, o, lse, wqkv, wo)
    (own,) = send(HOME, [own])
    return own[None]


def solution(mesh):
    return jax.shard_map(
        on_device,
        mesh=mesh,
        in_specs=(
            P("section", "tile", None),
            P("section", None, None),
            P("section", None, None),
            P("section", None),
            P("tile", None),
            P("tile"),
        ),
        out_specs=P("section", "tile", None),
        check_vma=False,
    )
```

```python
import functools
import math

import jax
import jax.numpy as jnp
from jax import lax
from jax.experimental import pallas as pl
from jax.experimental.pallas import tpu as pltpu
from jax.sharding import PartitionSpec as P

HEADS = 12
HD = 128
D = 1536
TS = 384
HALF = TS // 2
THIRD = TS // 3
N_TILE = 16
N_SECTION = 8
PAIR = 2 * HD
PAIRS = HEADS // 2
SCALE = HD ** (-0.5) * math.log2(math.e)
OFF = -1e30
BOTH = ("section", "tile")
UNROLL = False
NEAR_VMEM = 14 * 2**20
FAR_VMEM = 14 * 2**20
NEAR_FLOPS = 0
FAR_FLOPS = 0


def normalize(hidden, gain):
    widened = hidden.astype(jnp.float32)
    square = jnp.mean(widened * widened, axis=-1, keepdims=True)
    return (widened * lax.rsqrt(square + 1e-06) * gain).astype(jnp.bfloat16)


def dot(a, b):
    return jnp.dot(a, b, preferred_element_type=jnp.float32)


def dot_t(a, b):
    return lax.dot_general(a, b, (((1,), (1,)), ((), ())), preferred_element_type=jnp.float32)


def columns(j, first=0):
    return pl.ds(pl.multiple_of(first + j * PAIR, PAIR), PAIR)


def near_kernel(which, count, flag_ref, own_ref, *refs):
    near_refs, (gain_ref, w_ref, _, q_ref, o_ref, lse_ref, normed, kept_k, kept_v) = refs[:count], refs[count:]
    normed[:TS, :] = normalize(own_ref[...], gain_ref[...])
    rows = TS // count
    for i, ref in enumerate(near_refs):
        normed[TS + i * rows : TS + (i + 1) * rows, :] = normalize(ref[...], gain_ref[...])
    bias = jnp.where(flag_ref[which] > 0, 0.0, OFF)
    lane = lax.broadcasted_iota(jnp.int32, lse_ref.shape, 1)
    lse_ref[...] = jnp.zeros_like(lse_ref)
    for head in range(2):
        kept_v[:, :, head * PAIR + HD : (head + 1) * PAIR] = jnp.ones((2, 2 * TS, HD), jnp.bfloat16)

    def project_q(j):
        q_ref[:, columns(j)] = (dot(normed[:TS, :], w_ref[:, columns(j)]) * SCALE).astype(jnp.bfloat16)

    def project_k(j, slot):
        kept_k[slot] = dot(normed[...], w_ref[:, columns(j, D)]).astype(jnp.bfloat16)

    def project_v(j, slot):
        v = dot(normed[...], w_ref[:, columns(j, 2 * D)]).astype(jnp.bfloat16)
        kept_v[slot, :, :HD] = v[:, :HD]
        kept_v[slot, :, PAIR : PAIR + HD] = v[:, HD:]

    def score(q, k, i):
        return dot_t(q[:, i * HD : (i + 1) * HD], k[:, i * HD : (i + 1) * HD])

    def weigh(s):
        s0, s1 = s[:, :TS], s[:, TS:]
        m = jnp.maximum(jnp.max(s0, axis=1, keepdims=True), jnp.max(s1, axis=1, keepdims=True) + bias)
        p0 = jnp.exp2(s0 - m).astype(jnp.bfloat16)
        p1 = jnp.exp2(s1 - (m - bias)).astype(jnp.bfloat16)
        return jnp.concatenate([p0, p1], axis=1), m

    def collect(p, m, v, j, i):
        mixed = dot(p, v[:, i * PAIR : (i + 1) * PAIR])
        total = mixed[:, HD:]
        first = pl.multiple_of(j * PAIR, PAIR) + i * HD
        o_ref[:, pl.ds(first, HD)] = mixed[:, :HD] / total
        lse_ref[...] = jnp.where(lane == 2 * j + i, m + jnp.log2(total), lse_ref[...])

    project_q(0)
    project_k(0, 0)
    project_v(0, 0)

    def step(j, more):
        slot = j % 2
        q, k, v = q_ref[:, columns(j)], kept_k[slot], kept_v[slot]
        s0 = score(q, k, 0)
        if more:
            project_q(j + 1)
        p0, m0 = weigh(s0)
        s1 = score(q, k, 1)
        if more:
            project_k(j + 1, 1 - slot)
        p1, m1 = weigh(s1)
        collect(p0, m0, v, j, 0)
        if more:
            project_v(j + 1, 1 - slot)
        collect(p1, m1, v, j, 1)

    steps(step)


def steps(step):
    if UNROLL:
        for j in range(PAIRS - 1):
            step(j, True)
    else:
        lax.fori_loop(0, PAIRS - 1, lambda j, carry: step(j, True) or carry, 0)
    step(PAIRS - 1, False)


def far_kernel(which, count, flag_ref, own_ref, *refs):
    far_refs, refs = refs[:count], refs[count:]
    gain_ref, q_ref, o_ref, lse_ref, w_ref, wo_ref, out_ref, normed, mixed, kept_k, kept_v = refs
    rows = TS // count
    for i, ref in enumerate(far_refs):
        normed[i * rows : (i + 1) * rows, :] = normalize(ref[...], gain_ref[...])
    bias = jnp.where(flag_ref[which] > 0, 0.0, OFF)
    lane = lax.broadcasted_iota(jnp.int32, lse_ref.shape, 1)
    for head in range(2):
        kept_v[:, :, head * PAIR + HD : (head + 1) * PAIR] = jnp.ones((2, TS, HD), jnp.bfloat16)

    def project_k(j, slot):
        kept_k[slot] = dot(normed[...], w_ref[:, columns(j, D)]).astype(jnp.bfloat16)

    def project_v(j, slot):
        v = dot(normed[...], w_ref[:, columns(j, 2 * D)]).astype(jnp.bfloat16)
        kept_v[slot, :, :HD] = v[:, :HD]
        kept_v[slot, :, PAIR : PAIR + HD] = v[:, HD:]

    def score(q, k, i):
        return dot_t(q[:, i * HD : (i + 1) * HD], k[:, i * HD : (i + 1) * HD])

    def weigh(s):
        m = jnp.max(s, axis=1, keepdims=True)
        return jnp.exp2(s - m).astype(jnp.bfloat16), m + bias

    def collect(p, m, v, j, i):
        both = dot(p, v[:, i * PAIR : (i + 1) * PAIR])
        before = jnp.sum(jnp.where(lane == 2 * j + i, lse_ref[...], 0.0), axis=1, keepdims=True)
        top = jnp.maximum(before, m)
        w0, w1 = jnp.exp2(before - top), jnp.exp2(m - top)
        first = pl.multiple_of(j * PAIR, PAIR) + i * HD
        o = (o_ref[:, pl.ds(first, HD)] * w0 + both[:, :HD] * w1) / (w0 + both[:, HD:] * w1)
        mixed[:, pl.ds(first, HD)] = o.astype(jnp.bfloat16)

    project_k(0, 0)
    project_v(0, 0)

    def step(j, more):
        slot = j % 2
        q, k, v = q_ref[:, columns(j)], kept_k[slot], kept_v[slot]
        s0 = score(q, k, 0)
        s1 = score(q, k, 1)
        p0, m0 = weigh(s0)
        if more:
            project_k(j + 1, 1 - slot)
        p1, m1 = weigh(s1)
        collect(p0, m0, v, j, 0)
        if more:
            project_v(j + 1, 1 - slot)
        collect(p1, m1, v, j, 1)

    steps(step)

    def finish(j, carry):
        update = dot(mixed[...], wo_ref[:, columns(j)])
        out_ref[:, columns(j)] = (own_ref[:, columns(j)].astype(jnp.float32) + update).astype(jnp.bfloat16)
        return carry

    lax.fori_loop(0, PAIRS, finish, 0, unroll=UNROLL)


SMEM = pl.BlockSpec(memory_space=pltpu.SMEM)
VMEM = pl.BlockSpec(memory_space=pltpu.VMEM)


def near_attention(which, flags, own, near, gain, wqkv, wo):
    return pl.pallas_call(
        functools.partial(near_kernel, which, len(near)),
        out_shape=(
            jax.ShapeDtypeStruct((TS, D), jnp.bfloat16),
            jax.ShapeDtypeStruct((TS, D), jnp.float32),
            jax.ShapeDtypeStruct((TS, HD), jnp.float32),
        ),
        in_specs=[SMEM] + [VMEM] * (4 + len(near)),
        out_specs=(VMEM, VMEM, VMEM),
        scratch_shapes=[
            pltpu.VMEM((2 * TS, D), jnp.bfloat16),
            pltpu.VMEM((2, 2 * TS, PAIR), jnp.bfloat16),
            pltpu.VMEM((2, 2 * TS, 2 * PAIR), jnp.bfloat16),
        ],
        compiler_params=pltpu.CompilerParams(vmem_limit_bytes=NEAR_VMEM),
        cost_estimate=pl.CostEstimate(flops=NEAR_FLOPS, bytes_accessed=0, transcendentals=0),
        name="near_attention",
    )(flags, own, *near, gain, wqkv, wo)


def far_attention(which, flags, own, far, gain, q, o, lse, wqkv, wo):
    return pl.pallas_call(
        functools.partial(far_kernel, which, len(far)),
        out_shape=jax.ShapeDtypeStruct((TS, D), jnp.bfloat16),
        in_specs=[SMEM] + [VMEM] * (7 + len(far)),
        out_specs=VMEM,
        scratch_shapes=[
            pltpu.VMEM((TS, D), jnp.bfloat16),
            pltpu.VMEM((TS, D), jnp.bfloat16),
            pltpu.VMEM((2, TS, PAIR), jnp.bfloat16),
            pltpu.VMEM((2, TS, 2 * PAIR), jnp.bfloat16),
        ],
        compiler_params=pltpu.CompilerParams(vmem_limit_bytes=FAR_VMEM),
        cost_estimate=pl.CostEstimate(flops=FAR_FLOPS, bytes_accessed=0, transcendentals=0),
        name="far_attention",
    )(flags, own, *far, gain, q, o, lse, wqkv, wo)


def place(t):
    z, r = divmod(t, 4)
    if r == 0:
        return 4 * ((z - 1) % 4) + 1
    if r == 3:
        return 4 * z
    return 4 * z + 1 + r


def other(t):
    return t + 1 if t % 2 else t - 1


def route(moves):
    return [(s * N_TILE + a, (s + step) % N_SECTION * N_TILE + b) for s in range(N_SECTION) for step, a, b in moves]


def step_out(s):
    return s + 1 if s % 2 == 0 else s - 1


TILES = range(N_TILE)
CORE_SWAP = route([(0, t, t ^ 1) for t in TILES])
NEXT_CHIP = route([(0, t, other(t)) for t in TILES if 0 <= other(t) < N_TILE])
FORWARD = route([(1, t, place(t)) for t in TILES])
PAIR_OUT = [(s * N_TILE + t, step_out(s) * N_TILE + place(t ^ 1)) for s in range(N_SECTION) for t in TILES]
PAIR_IN = [(step_out(s) * N_TILE + u, (s + 1) % N_SECTION * N_TILE + u) for s in range(N_SECTION) for u in TILES]
HOME = route([(1, place(t), t) for t in TILES])
SPREAD = [(t, place(t)) for t in TILES]


def pieces(block, rows):
    return [block[i : i + rows] for i in range(0, TS, rows)]


def on_device(latents, wqkv, wo, gains, lists, counts):
    own = latents[0]
    wqkv, wo = wqkv[0], wo[0]

    def send(perm, blocks):
        return [lax.ppermute(block, BOTH, perm) for block in blocks]

    far = send(NEXT_CHIP, [own])
    near = send(CORE_SWAP, [own])
    tile = lax.axis_index("tile")
    pair = tile ^ 1
    beyond = jnp.where(tile % 2 == 1, tile + 1, tile - 1)
    used = jnp.arange(lists.shape[1]) < counts[0]
    pair_used = jnp.any((lists[0] == pair) & used).astype(jnp.int32)
    beyond_used = jnp.any((lists[0] == beyond) & used).astype(jnp.int32)
    flags = jnp.stack([pair_used, beyond_used])

    q, o, lse = near_attention(0, flags, own, near, gains, wqkv, wo)
    flags, lse = lax.optimization_barrier((flags, lse))
    flags_next = lax.ppermute(flags, "tile", SPREAD)
    flags, flags_next = lax.optimization_barrier((flags, flags_next))
    own = far_attention(1, flags, own, far, gains, q, o, lse, wqkv, wo)
    far = send(PAIR_IN, send(PAIR_OUT, pieces(own, HALF)))
    (own,) = send(FORWARD, [own])
    near = send(CORE_SWAP, pieces(own, THIRD))
    q, o, lse = near_attention(1, flags_next, own, near, gains, wqkv, wo)
    own = far_attention(0, flags_next, own, far, gains, q, o, lse, wqkv, wo)
    (own,) = send(HOME, [own])
    return own[None]


def solution(mesh):
    return jax.shard_map(
        on_device,
        mesh=mesh,
        in_specs=(
            P("section", "tile", None),
            P("section", None, None),
            P("section", None, None),
            P("section", None),
            P("tile", None),
            P("tile"),
        ),
        out_specs=P("section", "tile", None),
        check_vma=False,
    )
```

```python
import functools
import math

import jax
import jax.numpy as jnp
from jax import lax
from jax.experimental import pallas as pl
from jax.experimental.pallas import tpu as pltpu
from jax.sharding import PartitionSpec as P

HEADS = 12
HD = 128
D = 1536
TS = 384
HALF = TS // 2
THIRD = TS // 3
WIDE = 512
N_TILE = 16
N_SECTION = 8
PAIR = 2 * HD
PAIRS = HEADS // 2
SCALE = HD ** (-0.5) * math.log2(math.e)
OFF = -1e30
BOTH = ("section", "tile")
UNROLL = False
NEAR_VMEM = 14 * 2**20
FAR_VMEM = 14 * 2**20
NEAR_FLOPS = 0
FAR_FLOPS = 0


def normalize(hidden, gain):
    widened = hidden.astype(jnp.float32)
    square = jnp.mean(widened * widened, axis=-1, keepdims=True)
    return (widened * lax.rsqrt(square + 1e-06) * gain).astype(jnp.bfloat16)


def dot(a, b):
    return jnp.dot(a, b, preferred_element_type=jnp.float32)


def dot_t(a, b):
    return lax.dot_general(a, b, (((1,), (1,)), ((), ())), preferred_element_type=jnp.float32)


def columns(j, first=0):
    return pl.ds(pl.multiple_of(first + j * PAIR, PAIR), PAIR)


def switch(on):
    return jnp.where(on, 0.0, OFF)


def near_kernel(count, flag_ref, own_ref, *refs):
    near_refs, (gain_ref, w_ref, _, q_ref, o_ref, lse_ref, normed, kept_k, kept_v) = refs[:count], refs[count:]
    normed[:TS, :] = normalize(own_ref[:TS, :], gain_ref[...])
    rows = TS // count
    for i, ref in enumerate(near_refs):
        normed[TS + i * rows : TS + (i + 1) * rows, :] = normalize(ref[...], gain_ref[...])
    if own_ref.shape[0] > TS:
        bias = switch(own_ref[TS : TS + 8, :HD].astype(jnp.float32) > 0)[:1, :1]
    else:
        bias = switch(flag_ref[0] > 0)
    lane = lax.broadcasted_iota(jnp.int32, lse_ref.shape, 1)
    lse_ref[...] = jnp.zeros_like(lse_ref)
    for head in range(2):
        kept_v[:, :, head * PAIR + HD : (head + 1) * PAIR] = jnp.ones((2, 2 * TS, HD), jnp.bfloat16)

    def project_q(j):
        q_ref[:, columns(j)] = (dot(normed[:TS, :], w_ref[:, columns(j)]) * SCALE).astype(jnp.bfloat16)

    def project_k(j, slot):
        kept_k[slot] = dot(normed[...], w_ref[:, columns(j, D)]).astype(jnp.bfloat16)

    def project_v(j, slot):
        v = dot(normed[...], w_ref[:, columns(j, 2 * D)]).astype(jnp.bfloat16)
        kept_v[slot, :, :HD] = v[:, :HD]
        kept_v[slot, :, PAIR : PAIR + HD] = v[:, HD:]

    def score(q, k, i):
        return dot_t(q[:, i * HD : (i + 1) * HD], k[:, i * HD : (i + 1) * HD])

    def weigh(s):
        s0, s1 = s[:, :TS], s[:, TS:]
        m = jnp.maximum(jnp.max(s0, axis=1, keepdims=True), jnp.max(s1, axis=1, keepdims=True) + bias)
        p0 = jnp.exp2(s0 - m).astype(jnp.bfloat16)
        p1 = jnp.exp2(s1 - (m - bias)).astype(jnp.bfloat16)
        return jnp.concatenate([p0, p1], axis=1), m

    def collect(p, m, v, j, i):
        mixed = dot(p, v[:, i * PAIR : (i + 1) * PAIR])
        total = mixed[:, HD:]
        first = pl.multiple_of(j * PAIR, PAIR) + i * HD
        o_ref[:, pl.ds(first, HD)] = mixed[:, :HD] / total
        lse_ref[...] = jnp.where(lane == 2 * j + i, m + jnp.log2(total), lse_ref[...])

    project_q(0)
    project_k(0, 0)
    project_v(0, 0)

    def step(j, more):
        slot = j % 2
        q, k, v = q_ref[:, columns(j)], kept_k[slot], kept_v[slot]
        s0 = score(q, k, 0)
        if more:
            project_q(j + 1)
        p0, m0 = weigh(s0)
        s1 = score(q, k, 1)
        if more:
            project_k(j + 1, 1 - slot)
        p1, m1 = weigh(s1)
        collect(p0, m0, v, j, 0)
        if more:
            project_v(j + 1, 1 - slot)
        collect(p1, m1, v, j, 1)

    steps(step)


def steps(step):
    if UNROLL:
        for j in range(PAIRS - 1):
            step(j, True)
    else:
        lax.fori_loop(0, PAIRS - 1, lambda j, carry: step(j, True) or carry, 0)
    step(PAIRS - 1, False)


def far_kernel(count, flag_ref, own_ref, *refs):
    far_refs, refs = refs[:count], refs[count:]
    gain_ref, q_ref, o_ref, lse_ref, w_ref, wo_ref, out_ref, normed, mixed, kept_k, kept_v = refs
    rows = TS // count
    for i, ref in enumerate(far_refs):
        normed[i * rows : (i + 1) * rows, :] = normalize(ref[...], gain_ref[...])
    if own_ref.shape[0] > TS:
        bias = switch(own_ref[TS + 8 :, :HD].astype(jnp.float32) > 0)[:1, :1]
    else:
        bias = switch(flag_ref[1] > 0)
        out_ref[TS : TS + 8, :] = jnp.full((8, D), flag_ref[1], jnp.int32).astype(jnp.float32).astype(jnp.bfloat16)
        out_ref[TS + 8 :, :] = jnp.full((8, D), flag_ref[0], jnp.int32).astype(jnp.float32).astype(jnp.bfloat16)
    lane = lax.broadcasted_iota(jnp.int32, lse_ref.shape, 1)
    for head in range(2):
        kept_v[:, :, head * PAIR + HD : (head + 1) * PAIR] = jnp.ones((2, TS, HD), jnp.bfloat16)

    def project_k(j, slot):
        kept_k[slot] = dot(normed[...], w_ref[:, columns(j, D)]).astype(jnp.bfloat16)

    def project_v(j, slot):
        v = dot(normed[...], w_ref[:, columns(j, 2 * D)]).astype(jnp.bfloat16)
        kept_v[slot, :, :HD] = v[:, :HD]
        kept_v[slot, :, PAIR : PAIR + HD] = v[:, HD:]

    def score(q, k, i):
        return dot_t(q[:, i * HD : (i + 1) * HD], k[:, i * HD : (i + 1) * HD])

    def weigh(s):
        m = jnp.max(s, axis=1, keepdims=True)
        return jnp.exp2(s - m).astype(jnp.bfloat16), m + bias

    def collect(p, m, v, j, i):
        both = dot(p, v[:, i * PAIR : (i + 1) * PAIR])
        before = jnp.sum(jnp.where(lane == 2 * j + i, lse_ref[...], 0.0), axis=1, keepdims=True)
        top = jnp.maximum(before, m)
        w0, w1 = jnp.exp2(before - top), jnp.exp2(m - top)
        first = pl.multiple_of(j * PAIR, PAIR) + i * HD
        o = (o_ref[:, pl.ds(first, HD)] * w0 + both[:, :HD] * w1) / (w0 + both[:, HD:] * w1)
        mixed[:, pl.ds(first, HD)] = o.astype(jnp.bfloat16)

    project_k(0, 0)
    project_v(0, 0)

    def step(j, more):
        slot = j % 2
        q, k, v = q_ref[:, columns(j)], kept_k[slot], kept_v[slot]
        s0 = score(q, k, 0)
        s1 = score(q, k, 1)
        p0, m0 = weigh(s0)
        if more:
            project_k(j + 1, 1 - slot)
        p1, m1 = weigh(s1)
        collect(p0, m0, v, j, 0)
        if more:
            project_v(j + 1, 1 - slot)
        collect(p1, m1, v, j, 1)

    steps(step)

    def finish(j, carry):
        cut = pl.ds(pl.multiple_of(j * WIDE, WIDE), WIDE)
        update = dot(mixed[...], wo_ref[:, cut])
        out_ref[:TS, cut] = (own_ref[:TS, cut].astype(jnp.float32) + update).astype(jnp.bfloat16)
        return carry

    lax.fori_loop(0, D // WIDE, finish, 0)


SMEM = pl.BlockSpec(memory_space=pltpu.SMEM)
VMEM = pl.BlockSpec(memory_space=pltpu.VMEM)


def near_attention(flags, own, near, gain, wqkv, wo):
    return pl.pallas_call(
        functools.partial(near_kernel, len(near)),
        out_shape=(
            jax.ShapeDtypeStruct((TS, D), jnp.bfloat16),
            jax.ShapeDtypeStruct((TS, D), jnp.float32),
            jax.ShapeDtypeStruct((TS, HD), jnp.float32),
        ),
        in_specs=[SMEM] + [VMEM] * (4 + len(near)),
        out_specs=(VMEM, VMEM, VMEM),
        scratch_shapes=[
            pltpu.VMEM((2 * TS, D), jnp.bfloat16),
            pltpu.VMEM((2, 2 * TS, PAIR), jnp.bfloat16),
            pltpu.VMEM((2, 2 * TS, 2 * PAIR), jnp.bfloat16),
        ],
        compiler_params=pltpu.CompilerParams(vmem_limit_bytes=NEAR_VMEM),
        cost_estimate=pl.CostEstimate(flops=NEAR_FLOPS, bytes_accessed=0, transcendentals=0),
        name="near_attention",
    )(flags, own, *near, gain, wqkv, wo)


def far_attention(rows, flags, own, far, gain, q, o, lse, wqkv, wo):
    return pl.pallas_call(
        functools.partial(far_kernel, len(far)),
        out_shape=jax.ShapeDtypeStruct((rows, D), jnp.bfloat16),
        in_specs=[SMEM] + [VMEM] * (7 + len(far)),
        out_specs=VMEM,
        scratch_shapes=[
            pltpu.VMEM((TS, D), jnp.bfloat16),
            pltpu.VMEM((TS, D), jnp.bfloat16),
            pltpu.VMEM((2, TS, PAIR), jnp.bfloat16),
            pltpu.VMEM((2, TS, 2 * PAIR), jnp.bfloat16),
        ],
        compiler_params=pltpu.CompilerParams(vmem_limit_bytes=FAR_VMEM),
        cost_estimate=pl.CostEstimate(flops=FAR_FLOPS, bytes_accessed=0, transcendentals=0),
        name="far_attention",
    )(flags, own, *far, gain, q, o, lse, wqkv, wo)


def place(t):
    z, r = divmod(t, 4)
    if r == 0:
        return 4 * ((z - 1) % 4) + 1
    if r == 3:
        return 4 * z
    return 4 * z + 1 + r


def other(t):
    return t + 1 if t % 2 else t - 1


def route(moves):
    return [(s * N_TILE + a, (s + step) % N_SECTION * N_TILE + b) for s in range(N_SECTION) for step, a, b in moves]


def step_out(s):
    return s + 1 if s % 2 == 0 else s - 1


TILES = range(N_TILE)
CORE_SWAP = route([(0, t, t ^ 1) for t in TILES])
NEXT_CHIP = route([(0, t, other(t)) for t in TILES if 0 <= other(t) < N_TILE])
FORWARD = route([(1, t, place(t)) for t in TILES])
PAIR_OUT = [(s * N_TILE + t, step_out(s) * N_TILE + place(t ^ 1)) for s in range(N_SECTION) for t in TILES]
PAIR_IN = [(step_out(s) * N_TILE + u, (s + 1) % N_SECTION * N_TILE + u) for s in range(N_SECTION) for u in TILES]
HOME = route([(1, place(t), t) for t in TILES])


def pieces(block, rows):
    return [block[i : i + rows] for i in range(0, TS, rows)]


def on_device(latents, wqkv, wo, gains, lists, counts):
    own = latents[0]
    wqkv, wo = wqkv[0], wo[0]

    def send(perm, blocks):
        return [lax.ppermute(block, BOTH, perm) for block in blocks]

    far = send(NEXT_CHIP, [own])
    near = send(CORE_SWAP, [own])
    tile = lax.axis_index("tile")
    pair = tile ^ 1
    beyond = jnp.where(tile % 2 == 1, tile + 1, tile - 1)
    used = jnp.arange(lists.shape[1]) < counts[0]
    pair_used = jnp.any((lists[0] == pair) & used).astype(jnp.int32)
    beyond_used = jnp.any((lists[0] == beyond) & used).astype(jnp.int32)
    flags = jnp.stack([pair_used, beyond_used])

    q, o, lse = near_attention(flags, own, near, gains, wqkv, wo)
    own = far_attention(TS + 16, flags, own, far, gains, q, o, lse, wqkv, wo)
    far = send(PAIR_IN, send(PAIR_OUT, pieces(own, HALF)))
    (own,) = send(FORWARD, [own])
    near = send(CORE_SWAP, pieces(own, THIRD))
    q, o, lse = near_attention(flags, own, near, gains, wqkv, wo)
    own = far_attention(TS, flags, own, far, gains, q, o, lse, wqkv, wo)
    (own,) = send(HOME, [own])
    return own[None]


def solution(mesh):
    return jax.shard_map(
        on_device,
        mesh=mesh,
        in_specs=(
            P("section", "tile", None),
            P("section", None, None),
            P("section", None, None),
            P("section", None),
            P("tile", None),
            P("tile"),
        ),
        out_specs=P("section", "tile", None),
        check_vma=False,
    )
```

```python
import functools
import math

import jax
import jax.numpy as jnp
from jax import lax
from jax.experimental import pallas as pl
from jax.experimental.pallas import tpu as pltpu
from jax.sharding import PartitionSpec as P

HEADS = 12
HD = 128
D = 1536
TS = 384
NBR = 3
HALF = TS // 2
THIRD = TS // 3
WIDE = 512
N_TILE = 16
N_SECTION = 8
PAIR = 2 * HD
PAIRS = HEADS // 2
SCALE = HD ** (-0.5) * math.log2(math.e)
OFF = -1e30
BOTH = ("section", "tile")
UNROLL = False
NEAR_VMEM = 14 * 2**20
FAR_VMEM = 14 * 2**20
NEAR_FLOPS = 0
FAR_FLOPS = 0


def normalize(hidden, gain):
    widened = hidden.astype(jnp.float32)
    square = jnp.mean(widened * widened, axis=-1, keepdims=True)
    return (widened * lax.rsqrt(square + 1e-06) * gain).astype(jnp.bfloat16)


def dot(a, b):
    return jnp.dot(a, b, preferred_element_type=jnp.float32)


def dot_t(a, b):
    return lax.dot_general(a, b, (((1,), (1,)), ((), ())), preferred_element_type=jnp.float32)


def columns(j, first=0):
    return pl.ds(pl.multiple_of(first + j * PAIR, PAIR), PAIR)


def switch(on):
    return jnp.where(on, 0.0, OFF)


def uses(lists_ref, counts_ref):
    tile = lax.axis_index("tile")
    side = 2 * (tile % 2)

    def listed(neighbour):
        found = [(lists_ref[0, j] == neighbour) & (counts_ref[0] > j) for j in range(NBR)]
        return found[0] | found[1] | found[2]

    return listed(tile + 1 - side), listed(tile - 1 + side)


def guarded(run, turn):
    if turn is None:
        run()
    else:
        pl.when(lax.axis_index("section") % 2 == turn)(run)


def near_kernel(turn, count, lists_ref, counts_ref, own_ref, *refs):
    near_refs, (gain_ref, w_ref, _, q_ref, o_ref, lse_ref, normed, kept_k, kept_v) = refs[:count], refs[count:]

    def run():
        normed[:TS, :] = normalize(own_ref[:TS, :], gain_ref[...])
        rows = TS // count
        for i, ref in enumerate(near_refs):
            normed[TS + i * rows : TS + (i + 1) * rows, :] = normalize(ref[:rows, :], gain_ref[...])
        if own_ref.shape[0] > TS:
            bias = switch(own_ref[TS : TS + 8, :HD].astype(jnp.float32) > 0)[:1, :1]
        else:
            bias = switch(uses(lists_ref, counts_ref)[0])
        lane = lax.broadcasted_iota(jnp.int32, lse_ref.shape, 1)
        lse_ref[...] = jnp.zeros_like(lse_ref)
        for head in range(2):
            kept_v[:, :, head * PAIR + HD : (head + 1) * PAIR] = jnp.ones((2, 2 * TS, HD), jnp.bfloat16)

        def project_q(j):
            q_ref[:, columns(j)] = (dot(normed[:TS, :], w_ref[:, columns(j)]) * SCALE).astype(jnp.bfloat16)

        def project_k(j, slot):
            kept_k[slot] = dot(normed[...], w_ref[:, columns(j, D)]).astype(jnp.bfloat16)

        def project_v(j, slot):
            v = dot(normed[...], w_ref[:, columns(j, 2 * D)]).astype(jnp.bfloat16)
            kept_v[slot, :, :HD] = v[:, :HD]
            kept_v[slot, :, PAIR : PAIR + HD] = v[:, HD:]

        def score(q, k, i):
            return dot_t(q[:, i * HD : (i + 1) * HD], k[:, i * HD : (i + 1) * HD])

        def weigh(s):
            s0, s1 = s[:, :TS], s[:, TS:]
            m = jnp.maximum(jnp.max(s0, axis=1, keepdims=True), jnp.max(s1, axis=1, keepdims=True) + bias)
            p0 = jnp.exp2(s0 - m).astype(jnp.bfloat16)
            p1 = jnp.exp2(s1 - (m - bias)).astype(jnp.bfloat16)
            return jnp.concatenate([p0, p1], axis=1), m

        def collect(p, m, v, j, i):
            mixed = dot(p, v[:, i * PAIR : (i + 1) * PAIR])
            total = mixed[:, HD:]
            first = pl.multiple_of(j * PAIR, PAIR) + i * HD
            o_ref[:, pl.ds(first, HD)] = mixed[:, :HD] / total
            lse_ref[...] = jnp.where(lane == 2 * j + i, m + jnp.log2(total), lse_ref[...])

        project_q(0)
        project_k(0, 0)
        project_v(0, 0)

        def step(j, more):
            slot = j % 2
            q, k, v = q_ref[:, columns(j)], kept_k[slot], kept_v[slot]
            s0 = score(q, k, 0)
            if more:
                project_q(j + 1)
            p0, m0 = weigh(s0)
            s1 = score(q, k, 1)
            if more:
                project_k(j + 1, 1 - slot)
            p1, m1 = weigh(s1)
            collect(p0, m0, v, j, 0)
            if more:
                project_v(j + 1, 1 - slot)
            collect(p1, m1, v, j, 1)

        steps(step)

    guarded(run, turn)


def steps(step):
    if UNROLL:
        for j in range(PAIRS - 1):
            step(j, True)
    else:
        lax.fori_loop(0, PAIRS - 1, lambda j, carry: step(j, True) or carry, 0)
    step(PAIRS - 1, False)


def far_kernel(turn, count, lists_ref, counts_ref, own_ref, *refs):
    far_refs, refs = refs[:count], refs[count:]
    gain_ref, q_ref, o_ref, lse_ref, w_ref, wo_ref, out_ref, normed, mixed, kept_k, kept_v = refs

    def run():
        rows = TS // count
        for i, ref in enumerate(far_refs):
            normed[i * rows : (i + 1) * rows, :] = normalize(ref[:rows, :], gain_ref[...])
        if own_ref.shape[0] > TS:
            bias = switch(own_ref[TS + 8 :, :HD].astype(jnp.float32) > 0)[:1, :1]
        else:
            beside, beyond = uses(lists_ref, counts_ref)
            bias = switch(beyond)
            out_ref[TS : TS + 8, :] = jnp.full((8, D), jnp.where(beyond, 1.0, 0.0)).astype(jnp.bfloat16)
            out_ref[TS + 8 :, :] = jnp.full((8, D), jnp.where(beside, 1.0, 0.0)).astype(jnp.bfloat16)
        lane = lax.broadcasted_iota(jnp.int32, lse_ref.shape, 1)
        for head in range(2):
            kept_v[:, :, head * PAIR + HD : (head + 1) * PAIR] = jnp.ones((2, TS, HD), jnp.bfloat16)

        def project_k(j, slot):
            kept_k[slot] = dot(normed[...], w_ref[:, columns(j, D)]).astype(jnp.bfloat16)

        def project_v(j, slot):
            v = dot(normed[...], w_ref[:, columns(j, 2 * D)]).astype(jnp.bfloat16)
            kept_v[slot, :, :HD] = v[:, :HD]
            kept_v[slot, :, PAIR : PAIR + HD] = v[:, HD:]

        def score(q, k, i):
            return dot_t(q[:, i * HD : (i + 1) * HD], k[:, i * HD : (i + 1) * HD])

        def weigh(s):
            m = jnp.max(s, axis=1, keepdims=True)
            return jnp.exp2(s - m).astype(jnp.bfloat16), m + bias

        def collect(p, m, v, j, i):
            both = dot(p, v[:, i * PAIR : (i + 1) * PAIR])
            before = jnp.sum(jnp.where(lane == 2 * j + i, lse_ref[...], 0.0), axis=1, keepdims=True)
            top = jnp.maximum(before, m)
            w0, w1 = jnp.exp2(before - top), jnp.exp2(m - top)
            first = pl.multiple_of(j * PAIR, PAIR) + i * HD
            o = (o_ref[:, pl.ds(first, HD)] * w0 + both[:, :HD] * w1) / (w0 + both[:, HD:] * w1)
            mixed[:, pl.ds(first, HD)] = o.astype(jnp.bfloat16)

        project_k(0, 0)
        project_v(0, 0)

        def step(j, more):
            slot = j % 2
            q, k, v = q_ref[:, columns(j)], kept_k[slot], kept_v[slot]
            s0 = score(q, k, 0)
            s1 = score(q, k, 1)
            p0, m0 = weigh(s0)
            if more:
                project_k(j + 1, 1 - slot)
            p1, m1 = weigh(s1)
            collect(p0, m0, v, j, 0)
            if more:
                project_v(j + 1, 1 - slot)
            collect(p1, m1, v, j, 1)

        steps(step)

        def finish(j, carry):
            cut = pl.ds(pl.multiple_of(j * WIDE, WIDE), WIDE)
            update = dot(mixed[...], wo_ref[:, cut])
            out_ref[:TS, cut] = (own_ref[:TS, cut].astype(jnp.float32) + update).astype(jnp.bfloat16)
            return carry

        lax.fori_loop(0, D // WIDE, finish, 0)

    guarded(run, turn)


SMEM = pl.BlockSpec(memory_space=pltpu.SMEM)
VMEM = pl.BlockSpec(memory_space=pltpu.VMEM)
ANY = pl.BlockSpec(memory_space=pl.ANY)


def near_attention(turn, lists, counts, own, near, gain, wqkv, wo):
    return pl.pallas_call(
        functools.partial(near_kernel, turn, len(near)),
        out_shape=(
            jax.ShapeDtypeStruct((TS, D), jnp.bfloat16),
            jax.ShapeDtypeStruct((TS, D), jnp.float32),
            jax.ShapeDtypeStruct((TS, HD), jnp.float32),
        ),
        in_specs=[SMEM, SMEM] + [VMEM] * (4 + len(near)),
        out_specs=(VMEM, VMEM, VMEM),
        scratch_shapes=[
            pltpu.VMEM((2 * TS, D), jnp.bfloat16),
            pltpu.VMEM((2, 2 * TS, PAIR), jnp.bfloat16),
            pltpu.VMEM((2, 2 * TS, 2 * PAIR), jnp.bfloat16),
        ],
        compiler_params=pltpu.CompilerParams(vmem_limit_bytes=NEAR_VMEM),
        cost_estimate=pl.CostEstimate(flops=NEAR_FLOPS, bytes_accessed=0, transcendentals=0),
        name="near_attention",
    )(lists, counts, own, *near, gain, wqkv, wo)


def far_attention(turn, rows, lists, counts, own, far, gain, q, o, lse, wqkv, wo):
    return pl.pallas_call(
        functools.partial(far_kernel, turn, len(far)),
        out_shape=jax.ShapeDtypeStruct((rows, D), jnp.bfloat16),
        in_specs=[SMEM, SMEM] + [VMEM] * (7 + len(far)),
        out_specs=VMEM,
        scratch_shapes=[
            pltpu.VMEM((TS, D), jnp.bfloat16),
            pltpu.VMEM((TS, D), jnp.bfloat16),
            pltpu.VMEM((2, TS, PAIR), jnp.bfloat16),
            pltpu.VMEM((2, TS, 2 * PAIR), jnp.bfloat16),
        ],
        compiler_params=pltpu.CompilerParams(vmem_limit_bytes=FAR_VMEM),
        cost_estimate=pl.CostEstimate(flops=FAR_FLOPS, bytes_accessed=0, transcendentals=0),
        name="far_attention",
    )(lists, counts, own, *far, gain, q, o, lse, wqkv, wo)


def choose_kernel(a_ref, b_ref, out_ref, done):
    def move(source):
        copy = pltpu.make_async_copy(source, out_ref, done)
        copy.start()
        copy.wait()

    odd = lax.axis_index("section") % 2 == 1
    pl.when(odd)(lambda: move(b_ref))
    pl.when(jnp.logical_not(odd))(lambda: move(a_ref.at[pl.ds(0, TS)]))


def choose(a, b):
    return pl.pallas_call(
        choose_kernel,
        out_shape=jax.ShapeDtypeStruct((TS, D), jnp.bfloat16),
        in_specs=[VMEM, VMEM],
        out_specs=ANY,
        scratch_shapes=[pltpu.SemaphoreType.DMA],
        compiler_params=pltpu.CompilerParams(vmem_limit_bytes=NEAR_VMEM),
        name="choose",
    )(a, b)


def place(t):
    z, r = divmod(t, 4)
    if r == 0:
        return 4 * ((z - 1) % 4) + 1
    if r == 3:
        return 4 * z
    return 4 * z + 1 + r


def other(t):
    return t + 1 if t % 2 else t - 1


def route(moves, sections, step):
    return [(s * N_TILE + a, (s + step) % N_SECTION * N_TILE + b) for s in sections for a, b in moves]


TILES = range(N_TILE)
ALL, EVEN, ODD = range(N_SECTION), range(0, N_SECTION, 2), range(1, N_SECTION, 2)
SWAP = [(t, t ^ 1) for t in TILES]
SPREAD = [(t, place(t)) for t in TILES]
SPREAD_PAIR = [(t, place(t ^ 1)) for t in TILES]
STAY = [(t, t) for t in TILES]
GATHER = [(place(t), t) for t in TILES]
NEXT_CHIP = route([(t, other(t)) for t in TILES if 0 <= other(t) < N_TILE], ALL, 0)


def pieces(block, rows):
    return [block[i : i + rows] for i in range(0, TS, rows)]


def on_device(latents, wqkv, wo, gains, lists, counts):
    own = latents[0]
    wqkv, wo = wqkv[0], wo[0]

    def send(blocks, *route_of):
        perm = route(*route_of)
        return [lax.ppermute(block, BOTH, perm) for block in blocks]

    far = [lax.ppermute(own, BOTH, NEXT_CHIP)]
    near = send([own], SWAP, ALL, 0)
    q, o, lse = near_attention(None, lists, counts, own, near, gains, wqkv, wo)
    own = far_attention(None, TS + 16, lists, counts, own, far, gains, q, o, lse, wqkv, wo)

    (own_a,) = send([own], SPREAD, EVEN, 1)
    (own_b,) = send([own], SPREAD, ODD, 1)
    (turned,) = send([own], SPREAD_PAIR, ODD, -1)
    own, own_a = lax.optimization_barrier((own, own_a))
    far_a = send([own[:TS]], SPREAD_PAIR, EVEN, 1)

    near_a = send([own_a[:TS]], SWAP, ODD, 0)
    q, o, lse = near_attention(1, lists, counts, own_a, near_a, gains, wqkv, wo)
    turned, lse = lax.optimization_barrier((turned, lse))
    far_b = send([turned], STAY, EVEN, 2)
    done_a = far_attention(1, TS + 16, lists, counts, own_a, far_a, gains, q, o, lse, wqkv, wo)
    own_b, done_a = lax.optimization_barrier((own_b, done_a))
    (home_a,) = send([done_a], GATHER, ODD, 1)

    near_b = send([own_b[:TS]], SWAP, EVEN, 0)
    q, o, lse = near_attention(0, lists, counts, own_b, near_b, gains, wqkv, wo)
    done_b = far_attention(0, TS, lists, counts, own_b, far_b, gains, q, o, lse, wqkv, wo)
    (home_b,) = send([done_b], GATHER, EVEN, 1)
    return choose(home_a, home_b)[None]


def solution(mesh):
    return jax.shard_map(
        on_device,
        mesh=mesh,
        in_specs=(
            P("section", "tile", None),
            P("section", None, None),
            P("section", None, None),
            P("section", None),
            P("tile", None),
            P("tile"),
        ),
        out_specs=P("section", "tile", None),
        check_vma=False,
    )
```

```python
import functools
import math

import jax
import jax.numpy as jnp
from jax import lax
from jax.experimental import pallas as pl
from jax.experimental.pallas import tpu as pltpu
from jax.sharding import PartitionSpec as P

HEADS = 12
HD = 128
D = 1536
TS = 384
NBR = 3
HALF = TS // 2
THIRD = TS // 3
WIDE = 768
N_TILE = 16
N_SECTION = 8
PAIR = 2 * HD
PAIRS = HEADS // 2
SCALE = HD ** (-0.5) * math.log2(math.e)
OFF = -1e30
BOTH = ("section", "tile")
NEAR_VMEM = 14 * 2**20
FAR_VMEM = 14 * 2**20
NEAR_FLOPS = 0
FAR_FLOPS = 0


def normalize(hidden, gain):
    widened = hidden.astype(jnp.float32)
    square = jnp.mean(widened * widened, axis=-1, keepdims=True)
    return (widened * lax.rsqrt(square + 1e-06) * gain).astype(jnp.bfloat16)


def dot(a, b):
    return jnp.dot(a, b, preferred_element_type=jnp.float32)


def dot_t(a, b):
    return lax.dot_general(a, b, (((1,), (1,)), ((), ())), preferred_element_type=jnp.float32)


def columns(j, first=0):
    return pl.ds(pl.multiple_of(first + j * PAIR, PAIR), PAIR)


def switch(on):
    return jnp.where(on, 0.0, OFF)


def uses(lists_ref, counts_ref):
    tile = lax.axis_index("tile")
    side = 2 * (tile % 2)

    def listed(neighbour):
        found = [(lists_ref[0, j] == neighbour) & (counts_ref[0] > j) for j in range(NBR)]
        return found[0] | found[1] | found[2]

    return listed(tile + 1 - side), listed(tile - 1 + side)


def guarded(run, turn):
    if turn is None:
        run()
    else:
        pl.when(lax.axis_index("section") % 2 == turn)(run)


def near_kernel(turn, count, lists_ref, counts_ref, own_ref, *refs):
    near_refs, (gain_ref, w_ref, _, q_ref, o_ref, lse_ref, normed, kept_k, kept_v) = refs[:count], refs[count:]

    def run():
        normed[:TS, :] = normalize(own_ref[:TS, :], gain_ref[...])
        rows = TS // count
        for i, ref in enumerate(near_refs):
            normed[TS + i * rows : TS + (i + 1) * rows, :] = normalize(ref[:rows, :], gain_ref[...])
        if own_ref.shape[0] > TS:
            bias = switch(own_ref[TS : TS + 8, :HD].astype(jnp.float32) > 0)[:1, :1]
        else:
            bias = switch(uses(lists_ref, counts_ref)[0])
        lane = lax.broadcasted_iota(jnp.int32, lse_ref.shape, 1)
        lse_ref[...] = jnp.zeros_like(lse_ref)
        for head in range(2):
            kept_v[:, :, head * PAIR + HD : (head + 1) * PAIR] = jnp.ones((2, 2 * TS, HD), jnp.bfloat16)

        def project_q(j):
            q_ref[:, columns(j)] = (dot(normed[:TS, :], w_ref[:, columns(j)]) * SCALE).astype(jnp.bfloat16)

        def project_k(j, slot):
            kept_k[slot] = dot(normed[...], w_ref[:, columns(j, D)]).astype(jnp.bfloat16)

        def project_v(j, slot):
            v = dot(normed[...], w_ref[:, columns(j, 2 * D)]).astype(jnp.bfloat16)
            kept_v[slot, :, :HD] = v[:, :HD]
            kept_v[slot, :, PAIR : PAIR + HD] = v[:, HD:]

        def score(q, k, i):
            return dot_t(q[:, i * HD : (i + 1) * HD], k[:, i * HD : (i + 1) * HD])

        def weigh(s):
            s0, s1 = s[:, :TS], s[:, TS:]
            m = jnp.maximum(jnp.max(s0, axis=1, keepdims=True), jnp.max(s1, axis=1, keepdims=True) + bias)
            p0 = jnp.exp2(s0 - m).astype(jnp.bfloat16)
            p1 = jnp.exp2(s1 - (m - bias)).astype(jnp.bfloat16)
            return jnp.concatenate([p0, p1], axis=1), m

        def collect(p, m, v, j, i):
            mixed = dot(p, v[:, i * PAIR : (i + 1) * PAIR])
            total = mixed[:, HD:]
            first = pl.multiple_of(j * PAIR, PAIR) + i * HD
            o_ref[:, pl.ds(first, HD)] = mixed[:, :HD] / total
            lse_ref[...] = jnp.where(lane == 2 * j + i, m + jnp.log2(total), lse_ref[...])

        project_q(0)
        project_k(0, 0)
        project_v(0, 0)

        def step(j, more):
            slot = j % 2
            q, k, v = q_ref[:, columns(j)], kept_k[slot], kept_v[slot]
            s0 = score(q, k, 0)
            if more:
                project_q(j + 1)
            p0, m0 = weigh(s0)
            s1 = score(q, k, 1)
            if more:
                project_k(j + 1, 1 - slot)
            p1, m1 = weigh(s1)
            collect(p0, m0, v, j, 0)
            if more:
                project_v(j + 1, 1 - slot)
            collect(p1, m1, v, j, 1)

        steps(step, False)

    guarded(run, turn)


def steps(step, straight):
    if straight:
        for j in range(PAIRS - 1):
            step(j, True)
    else:
        lax.fori_loop(0, PAIRS - 1, lambda j, carry: step(j, True) or carry, 0)
    step(PAIRS - 1, False)


def far_kernel(turn, count, lists_ref, counts_ref, own_ref, *refs):
    far_refs, refs = refs[:count], refs[count:]
    gain_ref, q_ref, o_ref, lse_ref, w_ref, wo_ref, out_ref, normed, mixed, kept_k, kept_v = refs

    def run():
        rows = TS // count
        for i, ref in enumerate(far_refs):
            normed[i * rows : (i + 1) * rows, :] = normalize(ref[:rows, :], gain_ref[...])
        if own_ref.shape[0] > TS:
            bias = switch(own_ref[TS + 8 :, :HD].astype(jnp.float32) > 0)[:1, :1]
        else:
            beside, beyond = uses(lists_ref, counts_ref)
            bias = switch(beyond)
            out_ref[TS : TS + 8, :] = jnp.full((8, D), jnp.where(beyond, 1.0, 0.0)).astype(jnp.bfloat16)
            out_ref[TS + 8 :, :] = jnp.full((8, D), jnp.where(beside, 1.0, 0.0)).astype(jnp.bfloat16)
        lane = lax.broadcasted_iota(jnp.int32, lse_ref.shape, 1)
        for head in range(2):
            kept_v[:, :, head * PAIR + HD : (head + 1) * PAIR] = jnp.ones((2, TS, HD), jnp.bfloat16)

        def project_k(j, slot):
            kept_k[slot] = dot(normed[...], w_ref[:, columns(j, D)]).astype(jnp.bfloat16)

        def project_v(j, slot):
            v = dot(normed[...], w_ref[:, columns(j, 2 * D)]).astype(jnp.bfloat16)
            kept_v[slot, :, :HD] = v[:, :HD]
            kept_v[slot, :, PAIR : PAIR + HD] = v[:, HD:]

        def score(q, k, i):
            return dot_t(q[:, i * HD : (i + 1) * HD], k[:, i * HD : (i + 1) * HD])

        def weigh(s):
            m = jnp.max(s, axis=1, keepdims=True)
            return jnp.exp2(s - m).astype(jnp.bfloat16), m + bias

        def collect(p, m, v, j, i):
            both = dot(p, v[:, i * PAIR : (i + 1) * PAIR])
            before = jnp.sum(jnp.where(lane == 2 * j + i, lse_ref[...], 0.0), axis=1, keepdims=True)
            top = jnp.maximum(before, m)
            w0, w1 = jnp.exp2(before - top), jnp.exp2(m - top)
            first = pl.multiple_of(j * PAIR, PAIR) + i * HD
            o = (o_ref[:, pl.ds(first, HD)] * w0 + both[:, :HD] * w1) / (w0 + both[:, HD:] * w1)
            mixed[:, pl.ds(first, HD)] = o.astype(jnp.bfloat16)

        project_k(0, 0)
        project_v(0, 0)

        def step(j, more):
            slot = j % 2
            q, k, v = q_ref[:, columns(j)], kept_k[slot], kept_v[slot]
            s0 = score(q, k, 0)
            s1 = score(q, k, 1)
            p0, m0 = weigh(s0)
            if more:
                project_k(j + 1, 1 - slot)
            p1, m1 = weigh(s1)
            collect(p0, m0, v, j, 0)
            if more:
                project_v(j + 1, 1 - slot)
            collect(p1, m1, v, j, 1)

        steps(step, turn == 0)

        def finish(j, carry):
            cut = pl.ds(pl.multiple_of(j * WIDE, WIDE), WIDE)
            update = dot(mixed[...], wo_ref[:, cut])
            out_ref[:TS, cut] = (own_ref[:TS, cut].astype(jnp.float32) + update).astype(jnp.bfloat16)
            return carry

        lax.fori_loop(0, D // WIDE, finish, 0)

    guarded(run, turn)


SMEM = pl.BlockSpec(memory_space=pltpu.SMEM)
VMEM = pl.BlockSpec(memory_space=pltpu.VMEM)
ANY = pl.BlockSpec(memory_space=pl.ANY)


def near_attention(turn, lists, counts, own, near, gain, wqkv, wo):
    return pl.pallas_call(
        functools.partial(near_kernel, turn, len(near)),
        out_shape=(
            jax.ShapeDtypeStruct((TS, D), jnp.bfloat16),
            jax.ShapeDtypeStruct((TS, D), jnp.float32),
            jax.ShapeDtypeStruct((TS, HD), jnp.float32),
        ),
        in_specs=[SMEM, SMEM] + [VMEM] * (4 + len(near)),
        out_specs=(VMEM, VMEM, VMEM),
        scratch_shapes=[
            pltpu.VMEM((2 * TS, D), jnp.bfloat16),
            pltpu.VMEM((2, 2 * TS, PAIR), jnp.bfloat16),
            pltpu.VMEM((2, 2 * TS, 2 * PAIR), jnp.bfloat16),
        ],
        compiler_params=pltpu.CompilerParams(vmem_limit_bytes=NEAR_VMEM),
        cost_estimate=pl.CostEstimate(flops=NEAR_FLOPS, bytes_accessed=0, transcendentals=0),
        name="near_attention",
    )(lists, counts, own, *near, gain, wqkv, wo)


def far_attention(turn, rows, lists, counts, own, far, gain, q, o, lse, wqkv, wo):
    return pl.pallas_call(
        functools.partial(far_kernel, turn, len(far)),
        out_shape=jax.ShapeDtypeStruct((rows, D), jnp.bfloat16),
        in_specs=[SMEM, SMEM] + [VMEM] * (7 + len(far)),
        out_specs=VMEM,
        scratch_shapes=[
            pltpu.VMEM((TS, D), jnp.bfloat16),
            pltpu.VMEM((TS, D), jnp.bfloat16),
            pltpu.VMEM((2, TS, PAIR), jnp.bfloat16),
            pltpu.VMEM((2, TS, 2 * PAIR), jnp.bfloat16),
        ],
        compiler_params=pltpu.CompilerParams(vmem_limit_bytes=FAR_VMEM),
        cost_estimate=pl.CostEstimate(flops=FAR_FLOPS, bytes_accessed=0, transcendentals=0),
        name="far_attention",
    )(lists, counts, own, *far, gain, q, o, lse, wqkv, wo)


def choose_kernel(a_ref, b_ref, out_ref, done):
    def move(source):
        copy = pltpu.make_async_copy(source, out_ref, done)
        copy.start()
        copy.wait()

    odd = lax.axis_index("section") % 2 == 1
    pl.when(odd)(lambda: move(b_ref))
    pl.when(jnp.logical_not(odd))(lambda: move(a_ref.at[pl.ds(0, TS)]))


def choose(a, b):
    return pl.pallas_call(
        choose_kernel,
        out_shape=jax.ShapeDtypeStruct((TS, D), jnp.bfloat16),
        in_specs=[VMEM, VMEM],
        out_specs=ANY,
        scratch_shapes=[pltpu.SemaphoreType.DMA],
        compiler_params=pltpu.CompilerParams(vmem_limit_bytes=NEAR_VMEM),
        name="choose",
    )(a, b)


def place(t):
    z, r = divmod(t, 4)
    if r == 0:
        return 4 * ((z - 1) % 4) + 1
    if r == 3:
        return 4 * z
    return 4 * z + 1 + r


def other(t):
    return t + 1 if t % 2 else t - 1


def route(moves, sections, step):
    return [(s * N_TILE + a, (s + step) % N_SECTION * N_TILE + b) for s in sections for a, b in moves]


TILES = range(N_TILE)
ALL, EVEN, ODD = range(N_SECTION), range(0, N_SECTION, 2), range(1, N_SECTION, 2)
SWAP = [(t, t ^ 1) for t in TILES]
SPREAD = [(t, place(t)) for t in TILES]
SPREAD_PAIR = [(t, place(t ^ 1)) for t in TILES]
STAY = [(t, t) for t in TILES]
GATHER = [(place(t), t) for t in TILES]
NEXT_CHIP = route([(t, other(t)) for t in TILES if 0 <= other(t) < N_TILE], ALL, 0)


def pieces(block, rows):
    return [block[i : i + rows] for i in range(0, TS, rows)]


def on_device(latents, wqkv, wo, gains, lists, counts):
    own = latents[0]
    wqkv, wo = wqkv[0], wo[0]

    def send(blocks, *route_of):
        perm = route(*route_of)
        return [lax.ppermute(block, BOTH, perm) for block in blocks]

    far = [lax.ppermute(own, BOTH, NEXT_CHIP)]
    near = send([own], SWAP, ALL, 0)
    q, o, lse = near_attention(None, lists, counts, own, near, gains, wqkv, wo)
    own = far_attention(None, TS + 16, lists, counts, own, far, gains, q, o, lse, wqkv, wo)

    (own_a,) = send([own], SPREAD, EVEN, 1)
    (own_b,) = send([own], SPREAD, ODD, 1)
    (turned,) = send([own], SPREAD_PAIR, ODD, -1)
    own, own_a = lax.optimization_barrier((own, own_a))
    far_a = send([own[:TS]], SPREAD_PAIR, EVEN, 1)

    near_a = send([own_a[:TS]], SWAP, ODD, 0)
    q, o, lse = near_attention(1, lists, counts, own_a, near_a, gains, wqkv, wo)
    turned, lse = lax.optimization_barrier((turned, lse))
    far_b = send([turned], STAY, EVEN, 2)
    done_a = far_attention(1, TS + 16, lists, counts, own_a, far_a, gains, q, o, lse, wqkv, wo)
    own_b, done_a = lax.optimization_barrier((own_b, done_a))
    (home_a,) = send([done_a], GATHER, ODD, 1)

    near_b = send([own_b[:TS]], SWAP, EVEN, 0)
    q, o, lse = near_attention(0, lists, counts, own_b, near_b, gains, wqkv, wo)
    done_b = far_attention(0, TS, lists, counts, own_b, far_b, gains, q, o, lse, wqkv, wo)
    (home_b,) = send([done_b], GATHER, EVEN, 1)
    return choose(home_a, home_b)[None]


def solution(mesh):
    return jax.shard_map(
        on_device,
        mesh=mesh,
        in_specs=(
            P("section", "tile", None),
            P("section", None, None),
            P("section", None, None),
            P("section", None),
            P("tile", None),
            P("tile"),
        ),
        out_specs=P("section", "tile", None),
        check_vma=False,
    )
```

```python
import functools
import math

import jax
import jax.numpy as jnp
from jax import lax
from jax.experimental import pallas as pl
from jax.experimental.pallas import tpu as pltpu
from jax.sharding import PartitionSpec as P

HEADS = 12
HD = 128
D = 1536
TS = 384
NBR = 3
HALF = TS // 2
SHORT, LOOP, STRAIGHT = range(3)
THIRD = TS // 3
WIDE = 768
N_TILE = 16
N_SECTION = 8
PAIR = 2 * HD
PAIRS = HEADS // 2
SCALE = HD ** (-0.5) * math.log2(math.e)
OFF = -1e30
BOTH = ("section", "tile")
NEAR_VMEM = 14 * 2**20
FAR_VMEM = 14 * 2**20
NEAR_FLOPS = 0
FAR_FLOPS = 0


def normalize(hidden, gain):
    widened = hidden.astype(jnp.float32)
    square = jnp.mean(widened * widened, axis=-1, keepdims=True)
    return (widened * lax.rsqrt(square + 1e-06) * gain).astype(jnp.bfloat16)


def dot(a, b):
    return jnp.dot(a, b, preferred_element_type=jnp.float32)


def dot_t(a, b):
    return lax.dot_general(a, b, (((1,), (1,)), ((), ())), preferred_element_type=jnp.float32)


def columns(j, first=0):
    return pl.ds(pl.multiple_of(first + j * PAIR, PAIR), PAIR)


def switch(on):
    return jnp.where(on, 0.0, OFF)


def uses(lists_ref, counts_ref):
    tile = lax.axis_index("tile")
    side = 2 * (tile % 2)

    def listed(neighbour):
        found = [(lists_ref[0, j] == neighbour) & (counts_ref[0] > j) for j in range(NBR)]
        return found[0] | found[1] | found[2]

    return listed(tile + 1 - side), listed(tile - 1 + side)


def guarded(run, turn):
    if turn is None:
        run()
    else:
        pl.when(lax.axis_index("section") % 2 == turn)(run)


def near_kernel(turn, count, lists_ref, counts_ref, own_ref, *refs):
    near_refs, (gain_ref, w_ref, _, q_ref, o_ref, lse_ref, normed, kept_k, kept_v) = refs[:count], refs[count:]

    def run():
        normed[:TS, :] = normalize(own_ref[:TS, :], gain_ref[...])
        rows = TS // count
        for i, ref in enumerate(near_refs):
            normed[TS + i * rows : TS + (i + 1) * rows, :] = normalize(ref[:rows, :], gain_ref[...])
        if own_ref.shape[0] > TS:
            bias = switch(own_ref[TS : TS + 8, :HD].astype(jnp.float32) > 0)[:1, :1]
        else:
            bias = switch(uses(lists_ref, counts_ref)[0])
        lane = lax.broadcasted_iota(jnp.int32, lse_ref.shape, 1)
        lse_ref[...] = jnp.zeros_like(lse_ref)
        for head in range(2):
            kept_v[:, :, head * PAIR + HD : (head + 1) * PAIR] = jnp.ones((2, 2 * TS, HD), jnp.bfloat16)

        def project_q(j):
            q_ref[:, columns(j)] = (dot(normed[:TS, :], w_ref[:, columns(j)]) * SCALE).astype(jnp.bfloat16)

        def project_k(j, slot):
            kept_k[slot] = dot(normed[...], w_ref[:, columns(j, D)]).astype(jnp.bfloat16)

        def project_v(j, slot):
            v = dot(normed[...], w_ref[:, columns(j, 2 * D)]).astype(jnp.bfloat16)
            kept_v[slot, :, :HD] = v[:, :HD]
            kept_v[slot, :, PAIR : PAIR + HD] = v[:, HD:]

        def score(q, k, i):
            return dot_t(q[:, i * HD : (i + 1) * HD], k[:, i * HD : (i + 1) * HD])

        def weigh(s):
            s0, s1 = s[:, :TS], s[:, TS:]
            m = jnp.maximum(jnp.max(s0, axis=1, keepdims=True), jnp.max(s1, axis=1, keepdims=True) + bias)
            p0 = jnp.exp2(s0 - m).astype(jnp.bfloat16)
            p1 = jnp.exp2(s1 - (m - bias)).astype(jnp.bfloat16)
            return jnp.concatenate([p0, p1], axis=1), m

        def collect(p, m, v, j, i):
            mixed = dot(p, v[:, i * PAIR : (i + 1) * PAIR])
            total = mixed[:, HD:]
            first = pl.multiple_of(j * PAIR, PAIR) + i * HD
            o_ref[:, pl.ds(first, HD)] = mixed[:, :HD] / total
            lse_ref[...] = jnp.where(lane == 2 * j + i, m + jnp.log2(total), lse_ref[...])

        def project(j, slot):
            project_q(j)
            project_k(j, slot)
            project_v(j, slot)

        def step(j, more):
            slot = j % 2
            q, k, v = q_ref[:, columns(j)], kept_k[slot], kept_v[slot]
            s0 = score(q, k, 0)
            if more:
                project_q(j + 1)
            p0, m0 = weigh(s0)
            s1 = score(q, k, 1)
            if more:
                project_k(j + 1, 1 - slot)
            p1, m1 = weigh(s1)
            collect(p0, m0, v, j, 0)
            if more:
                project_v(j + 1, 1 - slot)
            collect(p1, m1, v, j, 1)

        steps(project, step, {None: SHORT, 1: SHORT, 0: LOOP}[turn])

    guarded(run, turn)


def steps(project, step, form):
    if form == SHORT:

        def both(j, carry):
            project(j, j % 2)
            step(j, False)
            return carry

        lax.fori_loop(0, PAIRS, both, 0)
        return
    project(0, 0)
    if form == STRAIGHT:
        for j in range(PAIRS - 1):
            step(j, True)
    else:
        lax.fori_loop(0, PAIRS - 1, lambda j, carry: step(j, True) or carry, 0)
    step(PAIRS - 1, False)


def far_kernel(turn, count, lists_ref, counts_ref, own_ref, *refs):
    far_refs, refs = refs[:count], refs[count:]
    gain_ref, q_ref, o_ref, lse_ref, w_ref, wo_ref, out_ref, normed, mixed, kept_k, kept_v = refs

    def run():
        rows = TS // count
        for i, ref in enumerate(far_refs):
            normed[i * rows : (i + 1) * rows, :] = normalize(ref[:rows, :], gain_ref[...])
        if own_ref.shape[0] > TS:
            bias = switch(own_ref[TS + 8 :, :HD].astype(jnp.float32) > 0)[:1, :1]
        else:
            beside, beyond = uses(lists_ref, counts_ref)
            bias = switch(beyond)
            out_ref[TS : TS + 8, :] = jnp.full((8, D), jnp.where(beyond, 1.0, 0.0)).astype(jnp.bfloat16)
            out_ref[TS + 8 :, :] = jnp.full((8, D), jnp.where(beside, 1.0, 0.0)).astype(jnp.bfloat16)
        lane = lax.broadcasted_iota(jnp.int32, lse_ref.shape, 1)
        for head in range(2):
            kept_v[:, :, head * PAIR + HD : (head + 1) * PAIR] = jnp.ones((2, TS, HD), jnp.bfloat16)

        def project_k(j, slot):
            kept_k[slot] = dot(normed[...], w_ref[:, columns(j, D)]).astype(jnp.bfloat16)

        def project_v(j, slot):
            v = dot(normed[...], w_ref[:, columns(j, 2 * D)]).astype(jnp.bfloat16)
            kept_v[slot, :, :HD] = v[:, :HD]
            kept_v[slot, :, PAIR : PAIR + HD] = v[:, HD:]

        def score(q, k, i):
            return dot_t(q[:, i * HD : (i + 1) * HD], k[:, i * HD : (i + 1) * HD])

        def weigh(s):
            m = jnp.max(s, axis=1, keepdims=True)
            return jnp.exp2(s - m).astype(jnp.bfloat16), m + bias

        def collect(p, m, v, j, i):
            both = dot(p, v[:, i * PAIR : (i + 1) * PAIR])
            before = jnp.sum(jnp.where(lane == 2 * j + i, lse_ref[...], 0.0), axis=1, keepdims=True)
            top = jnp.maximum(before, m)
            w0, w1 = jnp.exp2(before - top), jnp.exp2(m - top)
            first = pl.multiple_of(j * PAIR, PAIR) + i * HD
            o = (o_ref[:, pl.ds(first, HD)] * w0 + both[:, :HD] * w1) / (w0 + both[:, HD:] * w1)
            mixed[:, pl.ds(first, HD)] = o.astype(jnp.bfloat16)

        def project(j, slot):
            project_k(j, slot)
            project_v(j, slot)

        def step(j, more):
            slot = j % 2
            q, k, v = q_ref[:, columns(j)], kept_k[slot], kept_v[slot]
            s0 = score(q, k, 0)
            s1 = score(q, k, 1)
            p0, m0 = weigh(s0)
            if more:
                project_k(j + 1, 1 - slot)
            p1, m1 = weigh(s1)
            collect(p0, m0, v, j, 0)
            if more:
                project_v(j + 1, 1 - slot)
            collect(p1, m1, v, j, 1)

        steps(project, step, {None: STRAIGHT, 1: SHORT, 0: STRAIGHT}[turn])

        def finish(j, carry):
            cut = pl.ds(pl.multiple_of(j * WIDE, WIDE), WIDE)
            update = dot(mixed[...], wo_ref[:, cut])
            out_ref[:TS, cut] = (own_ref[:TS, cut].astype(jnp.float32) + update).astype(jnp.bfloat16)
            return carry

        lax.fori_loop(0, D // WIDE, finish, 0)

    guarded(run, turn)


SMEM = pl.BlockSpec(memory_space=pltpu.SMEM)
VMEM = pl.BlockSpec(memory_space=pltpu.VMEM)
ANY = pl.BlockSpec(memory_space=pl.ANY)


def near_attention(turn, lists, counts, own, near, gain, wqkv, wo):
    return pl.pallas_call(
        functools.partial(near_kernel, turn, len(near)),
        out_shape=(
            jax.ShapeDtypeStruct((TS, D), jnp.bfloat16),
            jax.ShapeDtypeStruct((TS, D), jnp.float32),
            jax.ShapeDtypeStruct((TS, HD), jnp.float32),
        ),
        in_specs=[SMEM, SMEM] + [VMEM] * (4 + len(near)),
        out_specs=(VMEM, VMEM, VMEM),
        scratch_shapes=[
            pltpu.VMEM((2 * TS, D), jnp.bfloat16),
            pltpu.VMEM((2, 2 * TS, PAIR), jnp.bfloat16),
            pltpu.VMEM((2, 2 * TS, 2 * PAIR), jnp.bfloat16),
        ],
        compiler_params=pltpu.CompilerParams(vmem_limit_bytes=NEAR_VMEM),
        cost_estimate=pl.CostEstimate(flops=NEAR_FLOPS, bytes_accessed=0, transcendentals=0),
        name="near_attention",
    )(lists, counts, own, *near, gain, wqkv, wo)


def far_attention(turn, rows, lists, counts, own, far, gain, q, o, lse, wqkv, wo):
    return pl.pallas_call(
        functools.partial(far_kernel, turn, len(far)),
        out_shape=jax.ShapeDtypeStruct((rows, D), jnp.bfloat16),
        in_specs=[SMEM, SMEM] + [VMEM] * (7 + len(far)),
        out_specs=VMEM,
        scratch_shapes=[
            pltpu.VMEM((TS, D), jnp.bfloat16),
            pltpu.VMEM((TS, D), jnp.bfloat16),
            pltpu.VMEM((2, TS, PAIR), jnp.bfloat16),
            pltpu.VMEM((2, TS, 2 * PAIR), jnp.bfloat16),
        ],
        compiler_params=pltpu.CompilerParams(vmem_limit_bytes=FAR_VMEM),
        cost_estimate=pl.CostEstimate(flops=FAR_FLOPS, bytes_accessed=0, transcendentals=0),
        name="far_attention",
    )(lists, counts, own, *far, gain, q, o, lse, wqkv, wo)


def choose_kernel(a_ref, b_ref, out_ref, done):
    def move(source):
        copy = pltpu.make_async_copy(source, out_ref, done)
        copy.start()
        copy.wait()

    odd = lax.axis_index("section") % 2 == 1
    pl.when(odd)(lambda: move(b_ref))
    pl.when(jnp.logical_not(odd))(lambda: move(a_ref.at[pl.ds(0, TS)]))


def choose(a, b):
    return pl.pallas_call(
        choose_kernel,
        out_shape=jax.ShapeDtypeStruct((TS, D), jnp.bfloat16),
        in_specs=[VMEM, VMEM],
        out_specs=ANY,
        scratch_shapes=[pltpu.SemaphoreType.DMA],
        compiler_params=pltpu.CompilerParams(vmem_limit_bytes=NEAR_VMEM),
        name="choose",
    )(a, b)


def place(t):
    z, r = divmod(t, 4)
    if r == 0:
        return 4 * ((z - 1) % 4) + 1
    if r == 3:
        return 4 * z
    return 4 * z + 1 + r


def other(t):
    return t + 1 if t % 2 else t - 1


def route(moves, sections, step):
    return [(s * N_TILE + a, (s + step) % N_SECTION * N_TILE + b) for s in sections for a, b in moves]


TILES = range(N_TILE)
ALL, EVEN, ODD = range(N_SECTION), range(0, N_SECTION, 2), range(1, N_SECTION, 2)
SWAP = [(t, t ^ 1) for t in TILES]
SPREAD = [(t, place(t)) for t in TILES]
SPREAD_PAIR = [(t, place(t ^ 1)) for t in TILES]
STAY = [(t, t) for t in TILES]
GATHER = [(place(t), t) for t in TILES]
NEXT_CHIP = route([(t, other(t)) for t in TILES if 0 <= other(t) < N_TILE], ALL, 0)


def pieces(block, rows):
    return [block[i : i + rows] for i in range(0, TS, rows)]


def on_device(latents, wqkv, wo, gains, lists, counts):
    own = latents[0]
    wqkv, wo = wqkv[0], wo[0]

    def send(blocks, *route_of):
        perm = route(*route_of)
        return [lax.ppermute(block, BOTH, perm) for block in blocks]

    far = [lax.ppermute(own, BOTH, NEXT_CHIP)]
    near = send([own], SWAP, ALL, 0)
    q, o, lse = near_attention(None, lists, counts, own, near, gains, wqkv, wo)
    own = far_attention(None, TS + 16, lists, counts, own, far, gains, q, o, lse, wqkv, wo)

    (own_a,) = send([own], SPREAD, EVEN, 1)
    (own_b,) = send([own], SPREAD, ODD, 1)
    (turned,) = send([own], SPREAD_PAIR, ODD, -1)
    own, own_a = lax.optimization_barrier((own, own_a))
    far_a = send([own[:TS]], SPREAD_PAIR, EVEN, 1)

    near_a = send([own_a[:TS]], SWAP, ODD, 0)
    q, o, lse = near_attention(1, lists, counts, own_a, near_a, gains, wqkv, wo)
    turned, lse = lax.optimization_barrier((turned, lse))
    far_b = send([turned], STAY, EVEN, 2)
    done_a = far_attention(1, TS + 16, lists, counts, own_a, far_a, gains, q, o, lse, wqkv, wo)
    own_b, done_a = lax.optimization_barrier((own_b, done_a))
    (home_a,) = send([done_a], GATHER, ODD, 1)

    near_b = send([own_b[:TS]], SWAP, EVEN, 0)
    q, o, lse = near_attention(0, lists, counts, own_b, near_b, gains, wqkv, wo)
    done_b = far_attention(0, TS, lists, counts, own_b, far_b, gains, q, o, lse, wqkv, wo)
    (home_b,) = send([done_b], GATHER, EVEN, 1)
    return choose(home_a, home_b)[None]


def solution(mesh):
    return jax.shard_map(
        on_device,
        mesh=mesh,
        in_specs=(
            P("section", "tile", None),
            P("section", None, None),
            P("section", None, None),
            P("section", None),
            P("tile", None),
            P("tile"),
        ),
        out_specs=P("section", "tile", None),
        check_vma=False,
    )
```
